32 devices in a mesh: group: 2 (over y), patch: 16 (over z, x, core).
Axes of the slice: x: 2, y: 2, z: 4, core: 2. Of those that a mesh axis runs over, the one named last changes fastest.
Arguments:
- strip_image: bfloat16 [2, 128, 128, 128], P('group', 'patch'), may hold values from -6 to 6
- strip_weight: bfloat16 [2, 128, 128, 128], P('group', 'patch'), may hold values from 0.25 to 4
- strip_patch: int32 [2, 128], P('group', 'patch'), may hold values from 0 to 15, as said below
- strip_slot: int32 [2, 128], P('group', 'patch'), may hold values from 0 to 7, as said below
- kernel_coef: float32 [2, 16, 2, 3, 31], P('group', 'patch'), may hold values from -5 to 5
Outputs:
- coadd: float32 [16, 128, 512], P('patch', 'group')
The draws below stay inside these ranges and needn't reach their ends.
Inputs may be any that keep to these rules, and one draw needn't show every extreme that they name: `strip_patch`: within a group, each device sends at most 1 of its strips to any one patch and sends exactly 1 to some patch; every patch receives exactly 8 strips of each group. `strip_slot`: within a group, the 8 strips on one patch carry each slot number once.
All inputs are finite; a program needn't handle non-finite values.
Results may differ from the reference program's by a relative error of at most 0.0051.
Values may be sent and summed in bfloat16 or wider, within the bound.
A program may use at most 128 MiB of HBM per device.

```python
import math
import jax
import jax.numpy as jnp
from jax import lax

NB = 31
TAPS = 23
HALF = 11
TERMS = 3
PATCH_ROWS = 128
PATCH_COLS = 512
STRIP_COLS = 128
BLOCKS = 4
VIS = 2
SD = 8
GROUPS = 2
PATCHES = 16
CAP = 1


def shuffle_slots(sub_key):
    return jax.random.permutation(sub_key, SD)


def route_group(group_key):
    key_profile, key_shift, key_slots, key_order = jax.random.split(group_key, 4)
    patch_axis = jnp.arange(PATCHES, dtype=jnp.int32)
    strip_axis = jnp.arange(SD, dtype=jnp.int32)
    full_count = SD // CAP
    remainder = SD % CAP
    base_counts = jnp.where(patch_axis < full_count, CAP, jnp.where(patch_axis == full_count, remainder, 0)).astype(jnp.int32)
    profile_counts = jax.random.permutation(key_profile, base_counts)
    source_shift = jax.random.permutation(key_shift, PATCHES).astype(jnp.int32)
    counts = profile_counts[(patch_axis[None, :] + source_shift[:, None]) % PATCHES]
    running_sum = jnp.cumsum(counts, axis=1)
    targets = jnp.sum((running_sum[:, None, :] <= strip_axis[None, :, None]).astype(jnp.int32), axis=2)
    pair_start = running_sum - counts
    local_rank = strip_axis[None, :] - jnp.take_along_axis(pair_start, targets, axis=1)
    column_start = jnp.cumsum(counts, axis=0) - counts
    arrival = jnp.take_along_axis(column_start, targets, axis=1) + local_rank
    slot_order = jax.vmap(shuffle_slots)(jax.random.split(key_slots, PATCHES)).astype(jnp.int32)
    labels = slot_order[targets, arrival]
    strip_order = jax.vmap(shuffle_slots)(jax.random.split(key_order, PATCHES)).astype(jnp.int32)
    targets = jnp.take_along_axis(targets, strip_order, axis=1)
    labels = jnp.take_along_axis(labels, strip_order, axis=1)
    return (targets.astype(jnp.int32), labels.astype(jnp.int32))


def route_table(key):
    group_keys = jax.random.split(jax.random.fold_in(key, 11), GROUPS)
    targets, labels = jax.vmap(route_group)(group_keys)
    return (targets.reshape(GROUPS, PATCHES * SD), labels.reshape(GROUPS, PATCHES * SD))


def draw_strip_patch(key, part):
    return route_table(key)[0]


def draw_strip_slot(key, part):
    return route_table(key)[1]


def shard_levels(stream_key, extent, shards, least, largest):
    factor_of, own = 1.0, jax.random.fold_in(stream_key, 6)
    for dim, shards_of in shards:
        heights = jnp.exp(jax.random.uniform(jax.random.fold_in(own, dim), (shards_of,), jnp.float32, least / len(shards), largest / len(shards)))
        factor_of = factor_of * jnp.repeat(heights, extent[dim] // shards_of).reshape([-1 if axis == dim else 1 for axis in range(len(extent))])
    return factor_of


def bell_draw(own_key, extent, width, most, cuts=(), kind=jnp.bfloat16):
    entries = width * jax.random.normal(own_key, extent, jnp.float32)
    if cuts:
        entries = entries * shard_levels(own_key, extent, cuts, -0.22, 0.18)
    return jnp.clip(entries, -most, most).astype(kind)


def setup_inputs(seed: int = 0) -> dict:
    key_of = jax.random.split(jax.random.key(seed), 6)
    strip_image = bell_draw(key_of[0], (GROUPS, PATCHES * SD, PATCH_ROWS, STRIP_COLS), 1.0, 6.0, ((0, 2), (1, 16)))
    strip_weight = jnp.clip(jnp.exp(math.log(4.0) - 2.7725887 * jax.random.uniform(key_of[1], (GROUPS, PATCHES * SD, PATCH_ROWS, STRIP_COLS), jnp.float32) ** shard_levels(key_of[1], (GROUPS, PATCHES * SD, PATCH_ROWS, STRIP_COLS), ((0, 2), (1, 16)), -0.2, 0.2)), 0.25, 4.0).astype(jnp.bfloat16)
    strip_patch = draw_strip_patch(jax.random.fold_in(key_of[5], 71), 0)
    strip_slot = draw_strip_slot(jax.random.fold_in(key_of[5], 71), 0)
    kernel_coef = bell_draw(key_of[4], (GROUPS, PATCHES, VIS, TERMS, NB), 1.0, 5.0, ((0, 2), (1, 16)), jnp.float32)
    return dict(strip_image=strip_image, strip_weight=strip_weight, strip_patch=strip_patch, strip_slot=strip_slot, kernel_coef=kernel_coef)


SPREADS = (0.7, 1.5, 3.0)
DEGREES = (4, 3, 2)

def profile_table(tap_count):
    half_width = (tap_count - 1) // 2
    offsets = jnp.arange(-half_width, half_width + 1).astype(jnp.float32)
    profiles = []
    for spread, degree in zip(SPREADS, DEGREES):
        for exponent in range(degree + 1):
            profile = jnp.exp(-offsets * offsets / (2.0 * spread * spread)) * (offsets / spread) ** exponent
            profiles.append(profile / jnp.sqrt(jnp.sum(profile * profile)))
    return jnp.stack(profiles).astype(jnp.float32)

def basis_pairs():
    vertical_list = []
    horizontal_list = []
    start_index = 0
    for degree in DEGREES:
        for vertical in range(degree + 1):
            for horizontal in range(degree + 1 - vertical):
                vertical_list.append(start_index + vertical)
                horizontal_list.append(start_index + horizontal)
        start_index += degree + 1
    return (vertical_list, horizontal_list)

def band_between(profile, inputs, outputs):
    half_width = (profile.shape[0] - 1) // 2
    differ = outputs[None, :] - inputs[:, None]
    inside = jnp.abs(differ) <= half_width
    picked = jnp.take(profile, jnp.clip(differ + half_width, 0, 2 * half_width).astype(jnp.int32), axis=0)
    return jnp.where(inside, picked, jnp.zeros_like(picked))

def reference(strip_image, strip_weight, strip_patch, strip_slot, kernel_coef):
    profiles = profile_table(TAPS).astype(jnp.bfloat16)
    profile_count = profiles.shape[0]
    vertical_list, horizontal_list = basis_pairs()
    vertical_index = jnp.asarray(vertical_list, dtype=jnp.int32)
    horizontal_index = jnp.asarray(horizontal_list, dtype=jnp.int32)
    row_axis = jnp.arange(PATCH_ROWS, dtype=jnp.int32)
    row_stack = jnp.concatenate([band_between(profiles[profile_index], row_axis, row_axis).T for profile_index in range(profile_count)], axis=0).astype(jnp.float32)
    col_taps = profiles[horizontal_index].astype(jnp.float32)
    flipped = col_taps[:, ::-1][:, None, :]
    across = (2.0 * jnp.arange(PATCH_COLS).astype(jnp.float32) - (PATCH_COLS - 1)) / (PATCH_COLS - 1)
    downward = (2.0 * jnp.arange(PATCH_ROWS).astype(jnp.float32) - (PATCH_ROWS - 1)) / (PATCH_ROWS - 1)

    def visit_term(visit_image, weight, visit_coef):
        row_pass = jnp.dot(row_stack, visit_image.astype(jnp.float32), precision=lax.Precision.HIGHEST)
        row_pass = row_pass.astype(jnp.bfloat16).reshape(profile_count, PATCH_ROWS, PATCH_COLS)
        chosen = row_pass[vertical_index].astype(jnp.float32)
        laid = jnp.transpose(chosen, (1, 0, 2))
        summed_conv = lax.conv_general_dilated(laid, flipped, (1,), [(HALF, HALF)], feature_group_count=NB, precision=lax.Precision.HIGHEST)
        summed_conv = jnp.transpose(summed_conv, (1, 0, 2))
        spatial = visit_coef[0][:, None, None] + visit_coef[1][:, None, None] * across[None, None, :] + visit_coef[2][:, None, None] * downward[None, :, None]
        picture = lax.optimization_barrier(jnp.sum(spatial * summed_conv, axis=0))
        inverse_var = weight.astype(jnp.float32)
        return (inverse_var * picture, inverse_var)

    def group_terms(group_index):
        images = strip_image[group_index]
        weights = strip_weight[group_index]
        targets = strip_patch[group_index]
        labels = strip_slot[group_index]
        ordering = jnp.argsort(targets * SD + labels).astype(jnp.int32)
        images = jnp.take(images, ordering, axis=0).reshape(PATCHES, VIS, BLOCKS, PATCH_ROWS, STRIP_COLS)
        weights = jnp.take(weights, ordering, axis=0).reshape(PATCHES, VIS, BLOCKS, PATCH_ROWS, STRIP_COLS)

        def patch_terms(packed):
            image_blocks, weight_blocks, coefs = packed

            def visit_step(running, visit_item):
                block_image, block_weight, visit_coef = visit_item
                visit_image = jnp.transpose(block_image, (1, 0, 2)).reshape(PATCH_ROWS, PATCH_COLS)
                weight = jnp.transpose(block_weight, (1, 0, 2)).reshape(PATCH_ROWS, PATCH_COLS)
                numerator, denominator = visit_term(visit_image, weight, visit_coef)
                return ((running[0] + numerator, running[1] + denominator), None)
            zeros_field = jnp.zeros((PATCH_ROWS, PATCH_COLS), jnp.float32)
            summed, _ = lax.scan(visit_step, (zeros_field, zeros_field), (image_blocks, weight_blocks, coefs))
            return summed
        return lax.map(patch_terms, (images, weights, kernel_coef[group_index]))

    def group_step(running, group_index):
        numerator, denominator = group_terms(group_index)
        return ((running[0] + numerator, running[1] + denominator), None)
    zeros_all = jnp.zeros((PATCHES, PATCH_ROWS, PATCH_COLS), jnp.float32)
    totals, _ = lax.scan(group_step, (zeros_all, zeros_all), jnp.arange(GROUPS, dtype=jnp.int32))
    return totals[0] / totals[1]
```

```python
import functools

import jax
import jax.numpy as jnp
import ml_dtypes
import numpy as np
from jax import lax
from jax.experimental import pallas as pl
from jax.experimental.pallas import tpu as pltpu
from jax.sharding import PartitionSpec as P

TAPS = 23
HALF = 11
SPREADS = (0.7, 1.5, 3.0)
DEGREES = (4, 3, 2)
MESH = pl.DeviceIdType.MESH
F32 = jnp.float32
BF16 = jnp.bfloat16


def profile_table():
    offsets = np.arange(-HALF, HALF + 1).astype(np.float64)
    profiles = []
    for spread, degree in zip(SPREADS, DEGREES):
        for power in range(degree + 1):
            profile = np.exp(-offsets * offsets / (2.0 * spread * spread)) * (offsets / spread) ** power
            profiles.append(profile / np.sqrt(np.sum(profile * profile)))
    return np.stack(profiles).astype(np.float32).astype(ml_dtypes.bfloat16).astype(np.float32)


def basis_pairs():
    pairs, start = [], 0
    for degree in DEGREES:
        for vertical in range(degree + 1):
            for horizontal in range(degree + 1 - vertical):
                pairs.append((start + vertical, start + horizontal))
        start += degree + 1
    return pairs


def band(profile, inputs, outputs):
    differ = outputs[None, :] - inputs[:, None]
    return np.where(np.abs(differ) <= HALF, profile[np.clip(differ + HALF, 0, 2 * HALF)], 0.0)


def tables(rows, width):
    profiles = profile_table()
    y = np.arange(rows)
    vertical = np.stack([band(p, y, y).T for p in profiles])
    x = np.arange(width)
    halo = np.where(x < width // 2, x + width, x - width)
    lanes = np.concatenate([x, halo])
    horizontal = np.concatenate([band(p, lanes, x) for p in profiles], axis=1)
    return vertical.astype(np.float32), horizontal.astype(ml_dtypes.bfloat16)


def kernel(
    groups, patches,
    patch_ref, slot_ref, coef_ref, img_hbm, wgt_hbm, ver_hbm, hor_hbm, out_ref,
    img_in, wgt_in, ver, band_h, img_send, img_recv, wgt_send, wgt_recv, lab_send, lab_recv,
    win, hor, mix, mat, mat_send, mat_recv,
    in_sem, lab_ssem, lab_rsem, fwd_ssem, fwd_rsem, img_ssem, img_rsem,
    wgt_ssem, wgt_osem, wgt_rsem, mat_ssem, mat_rsem,
):
    my_group, me = lax.axis_index("group"), lax.axis_index("patch")
    strips, rows, width = img_in.shape
    visits, cols = mat.shape[0], mat.shape[2]
    blocks = strips // visits
    slab = rows // groups
    count = ver.shape[0]
    devices = groups * patches

    loads = [
        pltpu.make_async_copy(src, dst, in_sem.at[i])
        for i, (src, dst) in enumerate(
            [(img_hbm.at[0], img_in), (wgt_hbm.at[0], wgt_in), (ver_hbm, ver), (hor_hbm, band_h)]
        )
    ]
    for load in loads:
        load.start()

    barrier = pltpu.get_barrier_semaphore()
    mine = my_group * patches + me

    def greet(i, carry):
        other = lax.rem(mine + 1 + i, devices)
        pl.semaphore_signal(
            barrier, inc=1, device_id=(other // patches, lax.rem(other, patches)), device_id_type=MESH
        )
        return carry

    lax.fori_loop(0, devices - 1, greet, 0)

    def source_of(p):
        source, label = jnp.int32(0), jnp.int32(0)
        for s in range(strips):
            here = patch_ref[0, s] == p
            source = jnp.where(here, s, source)
            label = jnp.where(here, slot_ref[0, s] + 1, label)
        return source, label

    def pack_label(p, carry):
        _, label = source_of(p)
        lab_send[p] = jnp.full((1, 128), label, jnp.int32)
        return carry

    def pack_image(p, carry):
        source, _ = source_of(p)
        img_send[p] = img_in[source]
        return carry

    def pack_weight(p, carry):
        source, _ = source_of(p)
        wgt_send[p] = wgt_in[source]
        return carry

    def other_patch(i):
        return lax.rem(me + 1 + lax.rem(i + patches // 4, patches - 1), patches)

    lax.fori_loop(0, patches, pack_label, 0)
    loads[0].wait()
    lax.fori_loop(0, patches, pack_image, 0)
    pl.semaphore_wait(barrier, devices - 1)

    def send_label(i, carry):
        p = other_patch(i)
        pltpu.make_async_remote_copy(
            src_ref=lab_send.at[p], dst_ref=lab_recv.at[my_group, me],
            send_sem=lab_ssem, recv_sem=lab_rsem, device_id=(my_group, p), device_id_type=MESH,
        ).start()
        return carry

    def send_image(i, carry):
        p = other_patch(i)
        pltpu.make_async_remote_copy(
            src_ref=img_send.at[p], dst_ref=img_recv.at[me],
            send_sem=img_ssem, recv_sem=img_rsem, device_id=(my_group, p), device_id_type=MESH,
        ).start()
        return carry

    lax.fori_loop(0, patches - 1, send_label, 0)
    pltpu.make_async_copy(lab_send.at[me], lab_recv.at[my_group, me], lab_rsem).start()
    lax.fori_loop(0, patches - 1, send_image, 0)
    pltpu.make_async_copy(img_send.at[me], img_recv.at[me], img_rsem).start()

    loads[1].wait()
    lax.fori_loop(0, patches, pack_weight, 0)

    loads[2].wait()
    pairs = basis_pairs()
    down = (2.0 * lax.broadcasted_iota(jnp.int32, (rows, rows), 0).astype(F32) - (rows - 1)) / (rows - 1)

    def mix_visit(v, carry):
        for r in range(count):
            flat = jnp.zeros((rows, rows), F32)
            across = jnp.zeros((rows, rows), F32)
            tilt = jnp.zeros((rows, rows), F32)
            for b, (q, h) in enumerate(pairs):
                if h == r:
                    vertical = ver[q]
                    flat = flat + coef_ref[v, 0, b] * vertical
                    across = across + coef_ref[v, 1, b] * vertical
                    tilt = tilt + coef_ref[v, 2, b] * vertical
            mix[v, :rows, r * rows : (r + 1) * rows] = (flat + down * tilt).astype(BF16)
            mix[v, rows:, r * rows : (r + 1) * rows] = across.astype(BF16)
        return carry

    lax.fori_loop(0, visits, mix_visit, 0)

    pltpu.make_async_copy(img_send.at[pl.ds(0, patches - 1)], img_send.at[pl.ds(0, patches - 1)], img_ssem).wait()

    def slab_of(g):
        return pl.ds(pl.multiple_of(g * slab, slab), slab)

    for d in range(groups):
        g = lax.rem(my_group + d, groups)

        def send_weight(i, carry, d=d, g=g):
            p = other_patch(i)
            pltpu.make_async_remote_copy(
                src_ref=wgt_send.at[p, slab_of(g)], dst_ref=wgt_recv.at[my_group, me],
                send_sem=wgt_osem if d == 0 else wgt_ssem, recv_sem=wgt_rsem,
                device_id=(g, p), device_id_type=MESH,
            ).start()
            return carry

        lax.fori_loop(0, patches - 1, send_weight, 0)
        if d == 0:
            pltpu.make_async_copy(wgt_send.at[me, slab_of(g)], wgt_recv.at[my_group, me], wgt_rsem).start()
        else:
            pltpu.make_async_remote_copy(
                src_ref=wgt_send.at[me, slab_of(g)], dst_ref=wgt_recv.at[my_group, me],
                send_sem=wgt_ssem, recv_sem=wgt_rsem, device_id=(g, me), device_id_type=MESH,
            ).start()

    pltpu.make_async_copy(lab_recv.at[0], lab_recv.at[0], lab_rsem).wait()
    for d in range(1, groups):
        pltpu.make_async_remote_copy(
            src_ref=lab_recv.at[my_group], dst_ref=lab_recv.at[my_group],
            send_sem=fwd_ssem, recv_sem=fwd_rsem,
            device_id=(lax.rem(my_group + d, groups), me), device_id_type=MESH,
        ).start()

    def positions(g):
        labels = lab_recv[g]
        order = lax.broadcasted_iota(jnp.int32, labels.shape, 0)
        return [
            jnp.max(jnp.where(labels == t + 1, order, 0)) for t in range(strips)
        ]

    place = positions(my_group)
    pltpu.make_async_copy(img_recv, img_recv, img_rsem).wait()

    zeros = jnp.zeros((rows, width), BF16)
    half = width // 2
    for t in range(strips):
        k = t % blocks
        here = slice(t * rows, (t + 1) * rows)
        win[here, :width] = img_recv[place[t]]
        right = img_recv[place[t + 1]] if k < blocks - 1 else zeros
        left = img_recv[place[t - 1]] if k > 0 else zeros
        win[here, width : width + half] = right[:, :half]
        win[here, width + half :] = left[:, half:]

    loads[3].wait()
    per = 2
    for v in range(visits):
        for j in range(count // per):
            part = jnp.dot(
                win[v * blocks * rows : (v + 1) * blocks * rows, :],
                band_h[:, j * per * width : (j + 1) * per * width],
                preferred_element_type=F32,
            ).astype(BF16)
            for k in range(blocks):
                for i in range(per):
                    r = j * per + i
                    hor[v, r * rows : (r + 1) * rows, k * width : (k + 1) * width] = part[
                        k * rows : (k + 1) * rows, i * width : (i + 1) * width
                    ]

    chunk = 2 * width
    for v in range(visits):
        for c in range(cols // chunk):
            here = slice(c * chunk, (c + 1) * chunk)
            both = jnp.dot(mix[v], hor[v, :, here], preferred_element_type=F32)
            at = lax.broadcasted_iota(jnp.int32, (rows, chunk), 1).astype(F32) + c * chunk
            sideways = (2.0 * at - (cols - 1)) / (cols - 1)
            matched = both[:rows] + sideways * both[rows:]
            mat[v, :, here] = matched
            mat_send[v, :, here] = matched.astype(BF16)
        for d in range(1, groups):
            g = lax.rem(my_group + d, groups)
            pltpu.make_async_remote_copy(
                src_ref=mat_send.at[v, slab_of(g)], dst_ref=mat_recv.at[my_group, v],
                send_sem=mat_ssem, recv_sem=mat_rsem, device_id=(g, me), device_id_type=MESH,
            ).start()

    rest = pl.ds(0, groups - 1)
    pltpu.make_async_copy(lab_recv.at[rest], lab_recv.at[rest], fwd_rsem).wait()
    places = [place]
    for d in range(1, groups):
        places.append(positions(lax.rem(my_group + d, groups)))
    pltpu.make_async_copy(mat_recv.at[rest], mat_recv.at[rest], mat_rsem).wait()
    pltpu.make_async_copy(wgt_recv, wgt_recv, wgt_rsem).wait()

    for k in range(blocks):
        here = slice(k * width, (k + 1) * width)
        numer = jnp.zeros((slab, width), F32)
        denom = jnp.zeros((slab, width), F32)
        for d in range(groups):
            g = lax.rem(my_group + d, groups)
            for v in range(visits):
                weight = wgt_recv[g, places[d][v * blocks + k]].astype(F32)
                if d == 0:
                    matched = mat[v, slab_of(my_group), here]
                else:
                    matched = mat_recv[g, v, :, here].astype(F32)
                numer = numer + weight * matched
                denom = denom + weight
        out_ref[0, :, here] = numer / denom

    some = pl.ds(0, patches - 1)
    pltpu.make_async_copy(lab_send.at[some], lab_send.at[some], lab_ssem).wait()
    pltpu.make_async_copy(lab_recv.at[rest], lab_recv.at[rest], fwd_ssem).wait()
    pltpu.make_async_copy(wgt_recv.at[0, some], wgt_recv.at[0, some], wgt_osem).wait()
    pltpu.make_async_copy(wgt_recv.at[rest], wgt_recv.at[rest], wgt_ssem).wait()
    pltpu.make_async_copy(mat_recv.at[rest], mat_recv.at[rest], mat_ssem).wait()


def solution(mesh):
    groups, patches = mesh.shape["group"], mesh.shape["patch"]

    def per_device(strip_image, strip_weight, strip_patch, strip_slot, kernel_coef):
        _, strips, rows, width = strip_image.shape
        visits = kernel_coef.shape[2]
        cols = strips // visits * width
        slab = rows // groups
        vertical, horizontal = tables(rows, width)
        count = vertical.shape[0]
        smem = pl.BlockSpec(memory_space=pltpu.SMEM)
        anywhere = pl.BlockSpec(memory_space=pl.ANY)
        dma = pltpu.SemaphoreType.DMA
        macs = visits * cols * rows * count * (2 * width + 2 * rows)
        return pl.pallas_call(
            functools.partial(kernel, groups, patches),
            out_shape=jax.ShapeDtypeStruct((1, slab, cols), F32),
            in_specs=[smem, smem, smem, anywhere, anywhere, anywhere, anywhere],
            out_specs=pl.BlockSpec(memory_space=pltpu.VMEM),
            scratch_shapes=[
                pltpu.VMEM((strips, rows, width), BF16),
                pltpu.VMEM((strips, rows, width), BF16),
                pltpu.VMEM(vertical.shape, F32),
                pltpu.VMEM(horizontal.shape, BF16),
                pltpu.VMEM((patches, rows, width), BF16),
                pltpu.VMEM((patches, rows, width), BF16),
                pltpu.VMEM((patches, rows, width), BF16),
                pltpu.VMEM((groups, patches, slab, width), BF16),
                pltpu.VMEM((patches, 1, 128), jnp.int32),
                pltpu.VMEM((groups, patches, 1, 128), jnp.int32),
                pltpu.VMEM((strips * rows, 2 * width), BF16),
                pltpu.VMEM((visits, count * rows, cols), BF16),
                pltpu.VMEM((visits, 2 * rows, count * rows), BF16),
                pltpu.VMEM((visits, rows, cols), F32),
                pltpu.VMEM((visits, rows, cols), BF16),
                pltpu.VMEM((groups, visits, slab, cols), BF16),
                dma((4,)),
            ]
            + [dma] * 11,
            compiler_params=pltpu.CompilerParams(
                collective_id=0, has_side_effects=True, vmem_limit_bytes=40 * 1024 * 1024
            ),
            cost_estimate=pl.CostEstimate(flops=2 * macs, bytes_accessed=1 << 21, transcendentals=0),
        )(
            strip_patch, strip_slot, kernel_coef[0, 0], strip_image, strip_weight,
            jnp.asarray(vertical), jnp.asarray(horizontal),
        )

    return jax.shard_map(
        per_device,
        mesh=mesh,
        in_specs=(
            P("group", "patch", None, None),
            P("group", "patch", None, None),
            P("group", "patch"),
            P("group", "patch"),
            P("group", "patch", None, None, None),
        ),
        out_specs=P("patch", "group", None),
        check_vma=False,
    )
```

```python
import functools

import jax
import jax.numpy as jnp
import ml_dtypes
import numpy as np
from jax import lax
from jax.experimental import pallas as pl
from jax.experimental.pallas import tpu as pltpu
from jax.sharding import PartitionSpec as P

TAPS = 23
HALF = 11
SPREADS = (0.7, 1.5, 3.0)
DEGREES = (4, 3, 2)
MESH = pl.DeviceIdType.MESH
F32 = jnp.float32
BF16 = jnp.bfloat16


def profile_table():
    offsets = np.arange(-HALF, HALF + 1).astype(np.float64)
    profiles = []
    for spread, degree in zip(SPREADS, DEGREES):
        for power in range(degree + 1):
            profile = np.exp(-offsets * offsets / (2.0 * spread * spread)) * (offsets / spread) ** power
            profiles.append(profile / np.sqrt(np.sum(profile * profile)))
    return np.stack(profiles).astype(np.float32).astype(ml_dtypes.bfloat16).astype(np.float32)


def basis_pairs():
    pairs, start = [], 0
    for degree in DEGREES:
        for vertical in range(degree + 1):
            for horizontal in range(degree + 1 - vertical):
                pairs.append((start + vertical, start + horizontal))
        start += degree + 1
    return pairs


def band(profile, inputs, outputs):
    differ = outputs[None, :] - inputs[:, None]
    return np.where(np.abs(differ) <= HALF, profile[np.clip(differ + HALF, 0, 2 * HALF)], 0.0)


def tables(rows, width):
    profiles = profile_table()
    y = np.arange(rows)
    vertical = np.stack([band(p, y, y).T for p in profiles])
    x = np.arange(width)
    halo = np.where(x < width // 2, x + width, x - width)
    lanes = np.concatenate([x, halo])
    horizontal = np.concatenate([band(p, lanes, x) for p in profiles], axis=1)
    return vertical.astype(np.float32), horizontal.astype(ml_dtypes.bfloat16)


def kernel(
    groups, patches,
    patch_hbm, slot_hbm, coef_hbm, img_hbm, wgt_hbm, ver_hbm, hor_hbm, out_ref,
    patch_ref, slot_ref, coef_ref,
    img_in, wgt_in, ver, band_h, img_send, img_recv, wgt_send, wgt_recv, lab_send, lab_recv,
    win, hor, mix, mat, mat_send, mat_recv,
    in_sem, lab_ssem, lab_rsem, fwd_ssem, fwd_rsem, img_ssem, img_rsem,
    wgt_ssem, wgt_osem, wgt_rsem, mat_ssem, mat_rsem,
):
    my_group, me = lax.axis_index("group"), lax.axis_index("patch")
    strips, rows, width = img_in.shape
    visits, cols = mat.shape[0], mat.shape[2]
    blocks = strips // visits
    slab = rows // groups
    count = ver.shape[0]
    devices = groups * patches

    loads = [
        pltpu.make_async_copy(src, dst, in_sem.at[i])
        for i, (src, dst) in enumerate(
            [
                (img_hbm.at[0], img_in), (wgt_hbm.at[0], wgt_in), (ver_hbm, ver), (hor_hbm, band_h),
                (patch_hbm, patch_ref), (slot_hbm, slot_ref), (coef_hbm, coef_ref),
            ]
        )
    ]
    for i in (4, 5, 0, 1, 6, 2, 3):
        loads[i].start()

    barrier = pltpu.get_barrier_semaphore()
    mine = my_group * patches + me

    def greet(i, carry):
        other = lax.rem(mine + 1 + i, devices)
        pl.semaphore_signal(
            barrier, inc=1, device_id=(other // patches, lax.rem(other, patches)), device_id_type=MESH
        )
        return carry

    lax.fori_loop(0, devices - 1, greet, 0)

    def source_of(p):
        source, label = jnp.int32(0), jnp.int32(0)
        for s in range(strips):
            here = patch_ref[0, s] == p
            source = jnp.where(here, s, source)
            label = jnp.where(here, slot_ref[0, s] + 1, label)
        return source, label

    def pack_label(p, carry):
        _, label = source_of(p)
        lab_send[p] = jnp.full((1, 128), label, jnp.int32)
        return carry

    def pack_image(p, carry):
        source, _ = source_of(p)
        img_send[p] = img_in[source]
        return carry

    def pack_weight(p, carry):
        source, _ = source_of(p)
        wgt_send[p] = wgt_in[source]
        return carry

    def other_patch(i):
        return lax.rem(me + 1 + lax.rem(i + patches // 4, patches - 1), patches)

    loads[4].wait()
    loads[5].wait()
    lax.fori_loop(0, patches, pack_label, 0)
    loads[0].wait()
    lax.fori_loop(0, patches, pack_image, 0)
    pl.semaphore_wait(barrier, devices - 1)

    def send_label(i, carry):
        p = other_patch(i)
        pltpu.make_async_remote_copy(
            src_ref=lab_send.at[p], dst_ref=lab_recv.at[my_group, me],
            send_sem=lab_ssem, recv_sem=lab_rsem, device_id=(my_group, p), device_id_type=MESH,
        ).start()
        return carry

    def send_image(i, carry):
        p = other_patch(i)
        pltpu.make_async_remote_copy(
            src_ref=img_send.at[p], dst_ref=img_recv.at[me],
            send_sem=img_ssem, recv_sem=img_rsem, device_id=(my_group, p), device_id_type=MESH,
        ).start()
        return carry

    lax.fori_loop(0, patches - 1, send_label, 0)
    pltpu.make_async_copy(lab_send.at[me], lab_recv.at[my_group, me], lab_rsem).start()
    lax.fori_loop(0, patches - 1, send_image, 0)
    pltpu.make_async_copy(img_send.at[me], img_recv.at[me], img_rsem).start()

    loads[1].wait()
    lax.fori_loop(0, patches, pack_weight, 0)

    loads[2].wait()
    loads[6].wait()
    pairs = basis_pairs()
    down = (2.0 * lax.broadcasted_iota(jnp.int32, (rows, rows), 0).astype(F32) - (rows - 1)) / (rows - 1)

    def mix_visit(v, carry):
        for r in range(count):
            flat = jnp.zeros((rows, rows), F32)
            across = jnp.zeros((rows, rows), F32)
            tilt = jnp.zeros((rows, rows), F32)
            for b, (q, h) in enumerate(pairs):
                if h == r:
                    vertical = ver[q]
                    flat = flat + coef_ref[0, v, b] * vertical
                    across = across + coef_ref[1, v, b] * vertical
                    tilt = tilt + coef_ref[2, v, b] * vertical
            mix[v, :rows, r * rows : (r + 1) * rows] = (flat + down * tilt).astype(BF16)
            mix[v, rows:, r * rows : (r + 1) * rows] = across.astype(BF16)
        return carry

    lax.fori_loop(0, visits, mix_visit, 0)

    pltpu.make_async_copy(img_send.at[pl.ds(0, patches - 1)], img_send.at[pl.ds(0, patches - 1)], img_ssem).wait()

    def slab_of(g):
        return pl.ds(pl.multiple_of(g * slab, slab), slab)

    for d in range(groups):
        g = lax.rem(my_group + d, groups)

        def send_weight(i, carry, d=d, g=g):
            p = other_patch(i)
            pltpu.make_async_remote_copy(
                src_ref=wgt_send.at[p, slab_of(g)], dst_ref=wgt_recv.at[my_group, me],
                send_sem=wgt_osem if d == 0 else wgt_ssem, recv_sem=wgt_rsem,
                device_id=(g, p), device_id_type=MESH,
            ).start()
            return carry

        lax.fori_loop(0, patches - 1, send_weight, 0)
        if d == 0:
            pltpu.make_async_copy(wgt_send.at[me, slab_of(g)], wgt_recv.at[my_group, me], wgt_rsem).start()
        else:
            pltpu.make_async_remote_copy(
                src_ref=wgt_send.at[me, slab_of(g)], dst_ref=wgt_recv.at[my_group, me],
                send_sem=wgt_ssem, recv_sem=wgt_rsem, device_id=(g, me), device_id_type=MESH,
            ).start()

    pltpu.make_async_copy(lab_recv.at[0], lab_recv.at[0], lab_rsem).wait()
    for d in range(1, groups):
        pltpu.make_async_remote_copy(
            src_ref=lab_recv.at[my_group], dst_ref=lab_recv.at[my_group],
            send_sem=fwd_ssem, recv_sem=fwd_rsem,
            device_id=(lax.rem(my_group + d, groups), me), device_id_type=MESH,
        ).start()

    def positions(g):
        labels = lab_recv[g]
        order = lax.broadcasted_iota(jnp.int32, labels.shape, 0)
        return [
            jnp.max(jnp.where(labels == t + 1, order, 0)) for t in range(strips)
        ]

    place = positions(my_group)
    pltpu.make_async_copy(img_recv, img_recv, img_rsem).wait()

    zeros = jnp.zeros((rows, width), BF16)
    half = width // 2
    for t in range(strips):
        k = t % blocks
        here = slice(t * rows, (t + 1) * rows)
        win[here, :width] = img_recv[place[t]]
        right = img_recv[place[t + 1]] if k < blocks - 1 else zeros
        left = img_recv[place[t - 1]] if k > 0 else zeros
        win[here, width : width + half] = right[:, :half]
        win[here, width + half :] = left[:, half:]

    loads[3].wait()
    per = 2
    for v in range(visits):
        for j in range(count // per):
            part = jnp.dot(
                win[v * blocks * rows : (v + 1) * blocks * rows, :],
                band_h[:, j * per * width : (j + 1) * per * width],
                preferred_element_type=F32,
            ).astype(BF16)
            for k in range(blocks):
                for i in range(per):
                    r = j * per + i
                    hor[v, r * rows : (r + 1) * rows, k * width : (k + 1) * width] = part[
                        k * rows : (k + 1) * rows, i * width : (i + 1) * width
                    ]

    chunk = 2 * width
    for v in range(visits):
        for c in range(cols // chunk):
            here = slice(c * chunk, (c + 1) * chunk)
            both = jnp.dot(mix[v], hor[v, :, here], preferred_element_type=F32)
            at = lax.broadcasted_iota(jnp.int32, (rows, chunk), 1).astype(F32) + c * chunk
            sideways = (2.0 * at - (cols - 1)) / (cols - 1)
            matched = both[:rows] + sideways * both[rows:]
            mat[v, :, here] = matched
            mat_send[v, :, here] = matched.astype(BF16)
        for d in range(1, groups):
            g = lax.rem(my_group + d, groups)
            pltpu.make_async_remote_copy(
                src_ref=mat_send.at[v, slab_of(g)], dst_ref=mat_recv.at[my_group, v],
                send_sem=mat_ssem, recv_sem=mat_rsem, device_id=(g, me), device_id_type=MESH,
            ).start()

    rest = pl.ds(0, groups - 1)
    pltpu.make_async_copy(lab_recv.at[rest], lab_recv.at[rest], fwd_rsem).wait()
    places = [place]
    for d in range(1, groups):
        places.append(positions(lax.rem(my_group + d, groups)))
    pltpu.make_async_copy(mat_recv.at[rest], mat_recv.at[rest], mat_rsem).wait()
    pltpu.make_async_copy(wgt_recv, wgt_recv, wgt_rsem).wait()

    for k in range(blocks):
        here = slice(k * width, (k + 1) * width)
        numer = jnp.zeros((slab, width), F32)
        denom = jnp.zeros((slab, width), F32)
        for d in range(groups):
            g = lax.rem(my_group + d, groups)
            for v in range(visits):
                weight = wgt_recv[g, places[d][v * blocks + k]].astype(F32)
                if d == 0:
                    matched = mat[v, slab_of(my_group), here]
                else:
                    matched = mat_recv[g, v, :, here].astype(F32)
                numer = numer + weight * matched
                denom = denom + weight
        out_ref[0, :, here] = numer / denom

    some = pl.ds(0, patches - 1)
    pltpu.make_async_copy(lab_send.at[some], lab_send.at[some], lab_ssem).wait()
    pltpu.make_async_copy(lab_recv.at[rest], lab_recv.at[rest], fwd_ssem).wait()
    pltpu.make_async_copy(wgt_recv.at[0, some], wgt_recv.at[0, some], wgt_osem).wait()
    pltpu.make_async_copy(wgt_recv.at[rest], wgt_recv.at[rest], wgt_ssem).wait()
    pltpu.make_async_copy(mat_recv.at[rest], mat_recv.at[rest], mat_ssem).wait()


def solution(mesh):
    groups, patches = mesh.shape["group"], mesh.shape["patch"]

    def per_device(strip_image, strip_weight, strip_patch, strip_slot, kernel_coef):
        _, strips, rows, width = strip_image.shape
        visits = kernel_coef.shape[2]
        cols = strips // visits * width
        slab = rows // groups
        vertical, horizontal = tables(rows, width)
        count = vertical.shape[0]
        far = pl.BlockSpec(memory_space=pltpu.HBM)
        coef = jnp.transpose(kernel_coef[0, 0], (1, 0, 2))
        dma = pltpu.SemaphoreType.DMA
        macs = visits * cols * rows * count * (2 * width + 2 * rows)
        return pl.pallas_call(
            functools.partial(kernel, groups, patches),
            out_shape=jax.ShapeDtypeStruct((1, slab, cols), F32),
            in_specs=[far] * 7,
            out_specs=pl.BlockSpec(memory_space=pltpu.VMEM),
            scratch_shapes=[
                pltpu.SMEM(strip_patch.shape, jnp.int32),
                pltpu.SMEM(strip_slot.shape, jnp.int32),
                pltpu.SMEM(coef.shape, F32),
                pltpu.VMEM((strips, rows, width), BF16),
                pltpu.VMEM((strips, rows, width), BF16),
                pltpu.VMEM(vertical.shape, F32),
                pltpu.VMEM(horizontal.shape, BF16),
                pltpu.VMEM((patches, rows, width), BF16),
                pltpu.VMEM((patches, rows, width), BF16),
                pltpu.VMEM((patches, rows, width), BF16),
                pltpu.VMEM((groups, patches, slab, width), BF16),
                pltpu.VMEM((patches, 1, 128), jnp.int32),
                pltpu.VMEM((groups, patches, 1, 128), jnp.int32),
                pltpu.VMEM((strips * rows, 2 * width), BF16),
                pltpu.VMEM((visits, count * rows, cols), BF16),
                pltpu.VMEM((visits, 2 * rows, count * rows), BF16),
                pltpu.VMEM((visits, rows, cols), F32),
                pltpu.VMEM((visits, rows, cols), BF16),
                pltpu.VMEM((groups, visits, slab, cols), BF16),
                dma((7,)),
            ]
            + [dma] * 11,
            compiler_params=pltpu.CompilerParams(
                collective_id=0, has_side_effects=True, vmem_limit_bytes=64 * 1024 * 1024
            ),
            cost_estimate=pl.CostEstimate(flops=2 * macs, bytes_accessed=1 << 21, transcendentals=0),
        )(
            strip_patch, strip_slot, coef, strip_image, strip_weight,
            jnp.asarray(vertical), jnp.asarray(horizontal),
        )

    return jax.shard_map(
        per_device,
        mesh=mesh,
        in_specs=(
            P("group", "patch", None, None),
            P("group", "patch", None, None),
            P("group", "patch"),
            P("group", "patch"),
            P("group", "patch", None, None, None),
        ),
        out_specs=P("patch", "group", None),
        check_vma=False,
    )
```

```python
import functools

import jax
import jax.numpy as jnp
import ml_dtypes
import numpy as np
from jax import lax
from jax.experimental import pallas as pl
from jax.experimental.pallas import tpu as pltpu
from jax.sharding import PartitionSpec as P

TAPS = 23
HALF = 11
SPREADS = (0.7, 1.5, 3.0)
DEGREES = (4, 3, 2)
MESH = pl.DeviceIdType.MESH
F32 = jnp.float32
BF16 = jnp.bfloat16


def profile_table():
    offsets = np.arange(-HALF, HALF + 1).astype(np.float64)
    profiles = []
    for spread, degree in zip(SPREADS, DEGREES):
        for power in range(degree + 1):
            profile = np.exp(-offsets * offsets / (2.0 * spread * spread)) * (offsets / spread) ** power
            profiles.append(profile / np.sqrt(np.sum(profile * profile)))
    return np.stack(profiles).astype(np.float32).astype(ml_dtypes.bfloat16).astype(np.float32)


def basis_pairs():
    pairs, start = [], 0
    for degree in DEGREES:
        for vertical in range(degree + 1):
            for horizontal in range(degree + 1 - vertical):
                pairs.append((start + vertical, start + horizontal))
        start += degree + 1
    return pairs


def band(profile, inputs, outputs):
    differ = outputs[None, :] - inputs[:, None]
    return np.where(np.abs(differ) <= HALF, profile[np.clip(differ + HALF, 0, 2 * HALF)], 0.0)


def tables(rows, width):
    profiles = profile_table()
    y = np.arange(rows)
    vertical = np.stack([band(p, y, y).T for p in profiles])
    x = np.arange(width)
    halo = np.where(x < width // 2, x + width, x - width)
    lanes = np.concatenate([x, halo])
    horizontal = np.concatenate([band(p, lanes, x) for p in profiles], axis=1)
    return vertical.astype(np.float32), horizontal.astype(ml_dtypes.bfloat16)


def kernel(
    groups, patches,
    patch_hbm, slot_hbm, coef_hbm, img_hbm, wgt_hbm, ver_hbm, hor_hbm, out_ref,
    patch_ref, slot_ref, coef_ref,
    img_in, wgt_in, ver, band_h, img_send, img_recv, wgt_send, wgt_recv, lab_send, lab_recv,
    win, hor, mix, mat, mat_send, mat_recv,
    in_sem, lab_ssem, lab_rsem, fwd_ssem, fwd_rsem, img_ssem, img_rsem,
    wgt_ssem, wgt_osem, wgt_rsem, mat_ssem, mat_rsem,
):
    my_group, me = lax.axis_index("group"), lax.axis_index("patch")
    strips, rows, width = img_in.shape
    visits, cols = mat.shape[0], mat.shape[2]
    blocks = strips // visits
    slab = rows // groups
    count = ver.shape[0]
    devices = groups * patches

    loads = [
        pltpu.make_async_copy(src, dst, in_sem.at[i])
        for i, (src, dst) in enumerate(
            [
                (img_hbm.at[0], img_in), (wgt_hbm.at[0], wgt_in), (ver_hbm, ver), (hor_hbm, band_h),
                (patch_hbm, patch_ref), (slot_hbm, slot_ref), (coef_hbm, coef_ref),
            ]
        )
    ]
    for i in (4, 5, 0, 1, 6, 2, 3):
        loads[i].start()

    barrier = pltpu.get_barrier_semaphore()
    mine = my_group * patches + me

    def greet(i, carry):
        other = lax.rem(mine + 1 + i, devices)
        pl.semaphore_signal(
            barrier, inc=1, device_id=(other // patches, lax.rem(other, patches)), device_id_type=MESH
        )
        return carry

    lax.fori_loop(0, devices - 1, greet, 0)

    def source_of(p):
        source, label = jnp.int32(0), jnp.int32(0)
        for s in range(strips):
            here = patch_ref[0, s] == p
            source = jnp.where(here, s, source)
            label = jnp.where(here, slot_ref[0, s] + 1, label)
        return source, label

    def pack_label(p, carry):
        _, label = source_of(p)
        lab_send[p] = jnp.full((1, 128), label, jnp.int32)
        return carry

    def pack_image(p, carry):
        source, _ = source_of(p)
        img_send[p] = img_in[source]
        return carry

    def pack_weight(p, carry):
        source, _ = source_of(p)
        wgt_send[p] = wgt_in[source]
        return carry

    def other_patch(i):
        return lax.rem(me + 1 + lax.rem(i + patches // 4, patches - 1), patches)

    loads[4].wait()
    loads[5].wait()
    lax.fori_loop(0, patches, pack_label, 0)
    loads[0].wait()
    lax.fori_loop(0, patches, pack_image, 0)
    pl.semaphore_wait(barrier, devices - 1)

    def send_label(i, carry):
        p = other_patch(i)
        pltpu.make_async_remote_copy(
            src_ref=lab_send.at[p], dst_ref=lab_recv.at[my_group, me],
            send_sem=lab_ssem, recv_sem=lab_rsem, device_id=(my_group, p), device_id_type=MESH,
        ).start()
        return carry

    def send_image(i, carry):
        p = other_patch(i)
        pltpu.make_async_remote_copy(
            src_ref=img_send.at[p], dst_ref=img_recv.at[me],
            send_sem=img_ssem, recv_sem=img_rsem, device_id=(my_group, p), device_id_type=MESH,
        ).start()
        return carry

    lax.fori_loop(0, patches - 1, send_label, 0)
    pltpu.make_async_copy(lab_send.at[me], lab_recv.at[my_group, me], lab_rsem).start()
    lax.fori_loop(0, patches - 1, send_image, 0)
    pltpu.make_async_copy(img_send.at[me], img_recv.at[me], img_rsem).start()

    loads[1].wait()
    lax.fori_loop(0, patches, pack_weight, 0)

    def slab_of(g):
        return pl.ds(pl.multiple_of(g * slab, slab), slab)

    for d in range(groups):
        g = lax.rem(my_group + d, groups)

        def send_weight(i, carry, d=d, g=g):
            p = other_patch(i)
            pltpu.make_async_remote_copy(
                src_ref=wgt_send.at[p, slab_of(g)], dst_ref=wgt_recv.at[my_group, me],
                send_sem=wgt_osem if d == 0 else wgt_ssem, recv_sem=wgt_rsem,
                device_id=(g, p), device_id_type=MESH,
            ).start()
            return carry

        lax.fori_loop(0, patches - 1, send_weight, 0)
        if d == 0:
            pltpu.make_async_copy(wgt_send.at[me, slab_of(g)], wgt_recv.at[my_group, me], wgt_rsem).start()
        else:
            pltpu.make_async_remote_copy(
                src_ref=wgt_send.at[me, slab_of(g)], dst_ref=wgt_recv.at[my_group, me],
                send_sem=wgt_ssem, recv_sem=wgt_rsem, device_id=(g, me), device_id_type=MESH,
            ).start()

    loads[2].wait()
    loads[6].wait()
    pairs = basis_pairs()
    down = (2.0 * lax.broadcasted_iota(jnp.int32, (rows, rows), 0).astype(F32) - (rows - 1)) / (rows - 1)

    def mix_visit(v, carry):
        for r in range(count):
            flat = jnp.zeros((rows, rows), F32)
            across = jnp.zeros((rows, rows), F32)
            tilt = jnp.zeros((rows, rows), F32)
            for b, (q, h) in enumerate(pairs):
                if h == r:
                    vertical = ver[q]
                    flat = flat + coef_ref[0, v, b] * vertical
                    across = across + coef_ref[1, v, b] * vertical
                    tilt = tilt + coef_ref[2, v, b] * vertical
            mix[v, :rows, r * rows : (r + 1) * rows] = (flat + down * tilt).astype(BF16)
            mix[v, rows:, r * rows : (r + 1) * rows] = across.astype(BF16)
        return carry

    lax.fori_loop(0, visits, mix_visit, 0)

    pltpu.make_async_copy(lab_recv.at[0], lab_recv.at[0], lab_rsem).wait()
    for d in range(1, groups):
        pltpu.make_async_remote_copy(
            src_ref=lab_recv.at[my_group], dst_ref=lab_recv.at[my_group],
            send_sem=fwd_ssem, recv_sem=fwd_rsem,
            device_id=(lax.rem(my_group + d, groups), me), device_id_type=MESH,
        ).start()

    def positions(g):
        labels = lab_recv[g]
        order = lax.broadcasted_iota(jnp.int32, labels.shape, 0)
        return [
            jnp.max(jnp.where(labels == t + 1, order, 0)) for t in range(strips)
        ]

    place = positions(my_group)
    pltpu.make_async_copy(img_recv, img_recv, img_rsem).wait()

    zeros = jnp.zeros((rows, width), BF16)
    half = width // 2
    for t in range(strips):
        k = t % blocks
        here = slice(t * rows, (t + 1) * rows)
        win[here, :width] = img_recv[place[t]]
        right = img_recv[place[t + 1]] if k < blocks - 1 else zeros
        left = img_recv[place[t - 1]] if k > 0 else zeros
        win[here, width : width + half] = right[:, :half]
        win[here, width + half :] = left[:, half:]

    loads[3].wait()
    per = 2
    for v in range(visits):
        for j in range(count // per):
            part = jnp.dot(
                win[v * blocks * rows : (v + 1) * blocks * rows, :],
                band_h[:, j * per * width : (j + 1) * per * width],
                preferred_element_type=F32,
            ).astype(BF16)
            for k in range(blocks):
                for i in range(per):
                    r = j * per + i
                    hor[v, r * rows : (r + 1) * rows, k * width : (k + 1) * width] = part[
                        k * rows : (k + 1) * rows, i * width : (i + 1) * width
                    ]

    chunk = 2 * width
    for v in range(visits):
        for c in range(cols // chunk):
            here = slice(c * chunk, (c + 1) * chunk)
            both = jnp.dot(mix[v], hor[v, :, here], preferred_element_type=F32)
            at = lax.broadcasted_iota(jnp.int32, (rows, chunk), 1).astype(F32) + c * chunk
            sideways = (2.0 * at - (cols - 1)) / (cols - 1)
            matched = both[:rows] + sideways * both[rows:]
            mat[v, :, here] = matched
            mat_send[v, :, here] = matched.astype(BF16)
        for d in range(1, groups):
            g = lax.rem(my_group + d, groups)
            pltpu.make_async_remote_copy(
                src_ref=mat_send.at[v, slab_of(g)], dst_ref=mat_recv.at[my_group, v],
                send_sem=mat_ssem, recv_sem=mat_rsem, device_id=(g, me), device_id_type=MESH,
            ).start()

    rest = pl.ds(0, groups - 1)
    pltpu.make_async_copy(lab_recv.at[rest], lab_recv.at[rest], fwd_rsem).wait()
    places = [place]
    for d in range(1, groups):
        places.append(positions(lax.rem(my_group + d, groups)))
    pltpu.make_async_copy(mat_recv.at[rest], mat_recv.at[rest], mat_rsem).wait()
    pltpu.make_async_copy(wgt_recv, wgt_recv, wgt_rsem).wait()

    for k in range(blocks):
        here = slice(k * width, (k + 1) * width)
        numer = jnp.zeros((slab, width), F32)
        denom = jnp.zeros((slab, width), F32)
        for d in range(groups):
            g = lax.rem(my_group + d, groups)
            for v in range(visits):
                weight = wgt_recv[g, places[d][v * blocks + k]].astype(F32)
                if d == 0:
                    matched = mat[v, slab_of(my_group), here]
                else:
                    matched = mat_recv[g, v, :, here].astype(F32)
                numer = numer + weight * matched
                denom = denom + weight
        out_ref[0, :, here] = numer / denom

    some = pl.ds(0, patches - 1)
    pltpu.make_async_copy(img_send.at[some], img_send.at[some], img_ssem).wait()
    pltpu.make_async_copy(lab_send.at[some], lab_send.at[some], lab_ssem).wait()
    pltpu.make_async_copy(lab_recv.at[rest], lab_recv.at[rest], fwd_ssem).wait()
    pltpu.make_async_copy(wgt_recv.at[0, some], wgt_recv.at[0, some], wgt_osem).wait()
    pltpu.make_async_copy(wgt_recv.at[rest], wgt_recv.at[rest], wgt_ssem).wait()
    pltpu.make_async_copy(mat_recv.at[rest], mat_recv.at[rest], mat_ssem).wait()


def solution(mesh):
    groups, patches = mesh.shape["group"], mesh.shape["patch"]

    def per_device(strip_image, strip_weight, strip_patch, strip_slot, kernel_coef):
        _, strips, rows, width = strip_image.shape
        visits = kernel_coef.shape[2]
        cols = strips // visits * width
        slab = rows // groups
        vertical, horizontal = tables(rows, width)
        count = vertical.shape[0]
        far = pl.BlockSpec(memory_space=pltpu.HBM)
        coef = jnp.transpose(kernel_coef[0, 0], (1, 0, 2))
        dma = pltpu.SemaphoreType.DMA
        macs = visits * cols * rows * count * (2 * width + 2 * rows)
        return pl.pallas_call(
            functools.partial(kernel, groups, patches),
            out_shape=jax.ShapeDtypeStruct((1, slab, cols), F32),
            in_specs=[far] * 7,
            out_specs=pl.BlockSpec(memory_space=pltpu.VMEM),
            scratch_shapes=[
                pltpu.SMEM(strip_patch.shape, jnp.int32),
                pltpu.SMEM(strip_slot.shape, jnp.int32),
                pltpu.SMEM(coef.shape, F32),
                pltpu.VMEM((strips, rows, width), BF16),
                pltpu.VMEM((strips, rows, width), BF16),
                pltpu.VMEM(vertical.shape, F32),
                pltpu.VMEM(horizontal.shape, BF16),
                pltpu.VMEM((patches, rows, width), BF16),
                pltpu.VMEM((patches, rows, width), BF16),
                pltpu.VMEM((patches, rows, width), BF16),
                pltpu.VMEM((groups, patches, slab, width), BF16),
                pltpu.VMEM((patches, 1, 128), jnp.int32),
                pltpu.VMEM((groups, patches, 1, 128), jnp.int32),
                pltpu.VMEM((strips * rows, 2 * width), BF16),
                pltpu.VMEM((visits, count * rows, cols), BF16),
                pltpu.VMEM((visits, 2 * rows, count * rows), BF16),
                pltpu.VMEM((visits, rows, cols), F32),
                pltpu.VMEM((visits, rows, cols), BF16),
                pltpu.VMEM((groups, visits, slab, cols), BF16),
                dma((7,)),
            ]
            + [dma] * 11,
            compiler_params=pltpu.CompilerParams(
                collective_id=0, has_side_effects=True, vmem_limit_bytes=64 * 1024 * 1024
            ),
            cost_estimate=pl.CostEstimate(flops=2 * macs, bytes_accessed=1 << 21, transcendentals=0),
        )(
            strip_patch, strip_slot, coef, strip_image, strip_weight,
            jnp.asarray(vertical), jnp.asarray(horizontal),
        )

    return jax.shard_map(
        per_device,
        mesh=mesh,
        in_specs=(
            P("group", "patch", None, None),
            P("group", "patch", None, None),
            P("group", "patch"),
            P("group", "patch"),
            P("group", "patch", None, None, None),
        ),
        out_specs=P("patch", "group", None),
        check_vma=False,
    )
```

```python
import functools

import jax
import jax.numpy as jnp
import ml_dtypes
import numpy as np
from jax import lax
from jax.experimental import pallas as pl
from jax.experimental.pallas import tpu as pltpu
from jax.sharding import PartitionSpec as P

TAPS = 23
HALF = 11
SPREADS = (0.7, 1.5, 3.0)
DEGREES = (4, 3, 2)
MESH = pl.DeviceIdType.MESH
F32 = jnp.float32
BF16 = jnp.bfloat16


def profile_table():
    offsets = np.arange(-HALF, HALF + 1).astype(np.float64)
    profiles = []
    for spread, degree in zip(SPREADS, DEGREES):
        for power in range(degree + 1):
            profile = np.exp(-offsets * offsets / (2.0 * spread * spread)) * (offsets / spread) ** power
            profiles.append(profile / np.sqrt(np.sum(profile * profile)))
    return np.stack(profiles).astype(np.float32).astype(ml_dtypes.bfloat16).astype(np.float32)


def basis_pairs():
    pairs, start = [], 0
    for degree in DEGREES:
        for vertical in range(degree + 1):
            for horizontal in range(degree + 1 - vertical):
                pairs.append((start + vertical, start + horizontal))
        start += degree + 1
    return pairs


def band(profile, inputs, outputs):
    differ = outputs[None, :] - inputs[:, None]
    return np.where(np.abs(differ) <= HALF, profile[np.clip(differ + HALF, 0, 2 * HALF)], 0.0)


def tables(rows, width):
    profiles = profile_table()
    y = np.arange(rows)
    vertical = np.stack([band(p, y, y).T for p in profiles])
    x = np.arange(width)
    halo = np.where(x < width // 2, x + width, x - width)
    lanes = np.concatenate([x, halo])
    horizontal = np.concatenate([band(p, lanes, x) for p in profiles], axis=1)
    return vertical.astype(np.float32), horizontal.astype(ml_dtypes.bfloat16)


def kernel(
    groups, patches,
    patch_hbm, slot_hbm, coef_hbm, img_hbm, wgt_hbm, ver_hbm, hor_hbm, out_ref,
    patch_ref, slot_ref, coef_ref,
    img_in, wgt_in, ver, band_h, img_send, img_recv, wgt_send, wgt_recv, lab_send, lab_recv,
    win, hor, mix, mat, mat_send, mat_recv,
    in_sem, lab_ssem, lab_rsem, fwd_ssem, fwd_rsem, img_fsem, img_ssem, img_rsem,
    wgt_ssem, wgt_osem, wgt_rsem, mat_ssem, mat_rsem,
):
    my_group, me = lax.axis_index("group"), lax.axis_index("patch")
    strips, rows, width = img_in.shape
    visits, cols = mat.shape[0], mat.shape[2]
    blocks = strips // visits
    slab = rows // groups
    count = ver.shape[0]
    devices = groups * patches

    loads = [
        pltpu.make_async_copy(src, dst, in_sem.at[i])
        for i, (src, dst) in enumerate(
            [
                (img_hbm.at[0], img_in), (wgt_hbm.at[0], wgt_in), (ver_hbm, ver), (hor_hbm, band_h),
                (patch_hbm, patch_ref), (slot_hbm, slot_ref), (coef_hbm, coef_ref),
            ]
        )
    ]
    for i in (4, 5, 0, 1, 6, 2, 3):
        loads[i].start()

    barrier = pltpu.get_barrier_semaphore()
    mine = my_group * patches + me

    def greet(i, carry):
        other = lax.rem(mine + 1 + i, devices)
        pl.semaphore_signal(
            barrier, inc=1, device_id=(other // patches, lax.rem(other, patches)), device_id_type=MESH
        )
        return carry

    lax.fori_loop(0, devices - 1, greet, 0)

    def source_of(p):
        source, label = jnp.int32(0), jnp.int32(0)
        for s in range(strips):
            here = patch_ref[0, s] == p
            source = jnp.where(here, s, source)
            label = jnp.where(here, slot_ref[0, s] + 1, label)
        return source, label

    def pack_label(p, carry):
        _, label = source_of(p)
        lab_send[p] = jnp.full((1, 128), label, jnp.int32)
        return carry

    def pack_image(p, carry):
        source, _ = source_of(p)
        img_send[p] = img_in[source]
        return carry

    def pack_weight(p, carry):
        source, _ = source_of(p)
        wgt_send[p] = wgt_in[source]
        return carry

    def other_patch(i):
        step = lax.select(lax.rem(i, 2) == 0, patches // 2 + lax.div(i, 2), lax.div(i + 1, 2))
        other, bit = jnp.int32(0), 1
        while bit < patches:
            other = other + bit * lax.rem(lax.div(me, bit) + lax.div(step, bit), 2)
            bit *= 2
        return other

    loads[4].wait()
    loads[5].wait()
    lax.fori_loop(0, patches, pack_label, 0)
    loads[0].wait()
    lax.fori_loop(0, patches, pack_image, 0)
    pl.semaphore_wait(barrier, devices - 1)

    def send_label(i, carry):
        p = other_patch(i)
        pltpu.make_async_remote_copy(
            src_ref=lab_send.at[p], dst_ref=lab_recv.at[my_group, me],
            send_sem=lab_ssem, recv_sem=lab_rsem, device_id=(my_group, p), device_id_type=MESH,
        ).start()
        return carry

    def send_image(i, carry, sem=img_ssem):
        p = other_patch(i)
        pltpu.make_async_remote_copy(
            src_ref=img_send.at[p], dst_ref=img_recv.at[me],
            send_sem=sem, recv_sem=img_rsem, device_id=(my_group, p), device_id_type=MESH,
        ).start()
        return carry

    first = patches // 2
    lax.fori_loop(0, first, functools.partial(send_image, sem=img_fsem), 0)
    lax.fori_loop(0, patches - 1, send_label, 0)
    pltpu.make_async_copy(lab_send.at[me], lab_recv.at[my_group, me], lab_rsem).start()
    lax.fori_loop(first, patches - 1, send_image, 0)
    pltpu.make_async_copy(img_send.at[me], img_recv.at[me], img_rsem).start()

    loads[1].wait()
    lax.fori_loop(0, patches, pack_weight, 0)

    loads[2].wait()
    loads[6].wait()
    pairs = basis_pairs()
    down = (2.0 * lax.broadcasted_iota(jnp.int32, (rows, rows), 0).astype(F32) - (rows - 1)) / (rows - 1)

    def mix_visit(v, carry):
        for r in range(count):
            flat = jnp.zeros((rows, rows), F32)
            across = jnp.zeros((rows, rows), F32)
            tilt = jnp.zeros((rows, rows), F32)
            for b, (q, h) in enumerate(pairs):
                if h == r:
                    vertical = ver[q]
                    flat = flat + coef_ref[0, v, b] * vertical
                    across = across + coef_ref[1, v, b] * vertical
                    tilt = tilt + coef_ref[2, v, b] * vertical
            mix[v, :rows, r * rows : (r + 1) * rows] = (flat + down * tilt).astype(BF16)
            mix[v, rows:, r * rows : (r + 1) * rows] = across.astype(BF16)
        return carry

    lax.fori_loop(0, visits, mix_visit, 0)

    pltpu.make_async_copy(img_send.at[pl.ds(0, first)], img_send.at[pl.ds(0, first)], img_fsem).wait()

    def slab_of(g):
        return pl.ds(pl.multiple_of(g * slab, slab), slab)

    def send_weight(i, carry):
        p = other_patch(i)
        for d in range(groups):
            g = lax.rem(my_group + d, groups)
            pltpu.make_async_remote_copy(
                src_ref=wgt_send.at[p, slab_of(g)], dst_ref=wgt_recv.at[my_group, me],
                send_sem=wgt_osem if d == 0 else wgt_ssem, recv_sem=wgt_rsem,
                device_id=(g, p), device_id_type=MESH,
            ).start()
        return carry

    lax.fori_loop(0, patches - 1, send_weight, 0)
    pltpu.make_async_copy(wgt_send.at[me, slab_of(my_group)], wgt_recv.at[my_group, me], wgt_rsem).start()
    for d in range(1, groups):
        g = lax.rem(my_group + d, groups)
        pltpu.make_async_remote_copy(
            src_ref=wgt_send.at[me, slab_of(g)], dst_ref=wgt_recv.at[my_group, me],
            send_sem=wgt_ssem, recv_sem=wgt_rsem, device_id=(g, me), device_id_type=MESH,
        ).start()

    pltpu.make_async_copy(lab_recv.at[0], lab_recv.at[0], lab_rsem).wait()
    for d in range(1, groups):
        pltpu.make_async_remote_copy(
            src_ref=lab_recv.at[my_group], dst_ref=lab_recv.at[my_group],
            send_sem=fwd_ssem, recv_sem=fwd_rsem,
            device_id=(lax.rem(my_group + d, groups), me), device_id_type=MESH,
        ).start()

    def positions(g):
        labels = lab_recv[g]
        order = lax.broadcasted_iota(jnp.int32, labels.shape, 0)
        return [
            jnp.max(jnp.where(labels == t + 1, order, 0)) for t in range(strips)
        ]

    place = positions(my_group)
    pltpu.make_async_copy(img_recv, img_recv, img_rsem).wait()

    zeros = jnp.zeros((rows, width), BF16)
    half = width // 2
    for t in range(strips):
        k = t % blocks
        here = slice(t * rows, (t + 1) * rows)
        win[here, :width] = img_recv[place[t]]
        right = img_recv[place[t + 1]] if k < blocks - 1 else zeros
        left = img_recv[place[t - 1]] if k > 0 else zeros
        win[here, width : width + half] = right[:, :half]
        win[here, width + half :] = left[:, half:]

    loads[3].wait()
    per = 2
    for v in range(visits):
        for j in range(count // per):
            part = jnp.dot(
                win[v * blocks * rows : (v + 1) * blocks * rows, :],
                band_h[:, j * per * width : (j + 1) * per * width],
                preferred_element_type=F32,
            ).astype(BF16)
            for k in range(blocks):
                for i in range(per):
                    r = j * per + i
                    hor[v, r * rows : (r + 1) * rows, k * width : (k + 1) * width] = part[
                        k * rows : (k + 1) * rows, i * width : (i + 1) * width
                    ]

    chunk = 2 * width
    for v in range(visits):
        for c in range(cols // chunk):
            here = slice(c * chunk, (c + 1) * chunk)
            both = jnp.dot(mix[v], hor[v, :, here], preferred_element_type=F32)
            at = lax.broadcasted_iota(jnp.int32, (rows, chunk), 1).astype(F32) + c * chunk
            sideways = (2.0 * at - (cols - 1)) / (cols - 1)
            matched = both[:rows] + sideways * both[rows:]
            mat[v, :, here] = matched
            mat_send[v, :, here] = matched.astype(BF16)
        for d in range(1, groups):
            g = lax.rem(my_group + d, groups)
            pltpu.make_async_remote_copy(
                src_ref=mat_send.at[v, slab_of(g)], dst_ref=mat_recv.at[my_group, v],
                send_sem=mat_ssem, recv_sem=mat_rsem, device_id=(g, me), device_id_type=MESH,
            ).start()

    rest = pl.ds(0, groups - 1)
    pltpu.make_async_copy(lab_recv.at[rest], lab_recv.at[rest], fwd_rsem).wait()
    places = [place]
    for d in range(1, groups):
        places.append(positions(lax.rem(my_group + d, groups)))
    pltpu.make_async_copy(mat_recv.at[rest], mat_recv.at[rest], mat_rsem).wait()
    pltpu.make_async_copy(wgt_recv, wgt_recv, wgt_rsem).wait()

    for k in range(blocks):
        here = slice(k * width, (k + 1) * width)
        numer = jnp.zeros((slab, width), F32)
        denom = jnp.zeros((slab, width), F32)
        for d in range(groups):
            g = lax.rem(my_group + d, groups)
            for v in range(visits):
                weight = wgt_recv[g, places[d][v * blocks + k]].astype(F32)
                if d == 0:
                    matched = mat[v, slab_of(my_group), here]
                else:
                    matched = mat_recv[g, v, :, here].astype(F32)
                numer = numer + weight * matched
                denom = denom + weight
        out_ref[0, :, here] = numer / denom

    some = pl.ds(0, patches - 1)
    last = pl.ds(0, patches - 1 - first)
    pltpu.make_async_copy(img_send.at[last], img_send.at[last], img_ssem).wait()
    pltpu.make_async_copy(lab_send.at[some], lab_send.at[some], lab_ssem).wait()
    pltpu.make_async_copy(lab_recv.at[rest], lab_recv.at[rest], fwd_ssem).wait()
    pltpu.make_async_copy(wgt_recv.at[0, some], wgt_recv.at[0, some], wgt_osem).wait()
    pltpu.make_async_copy(wgt_recv.at[rest], wgt_recv.at[rest], wgt_ssem).wait()
    pltpu.make_async_copy(mat_recv.at[rest], mat_recv.at[rest], mat_ssem).wait()


def solution(mesh):
    groups, patches = mesh.shape["group"], mesh.shape["patch"]

    def per_device(strip_image, strip_weight, strip_patch, strip_slot, kernel_coef):
        _, strips, rows, width = strip_image.shape
        visits = kernel_coef.shape[2]
        cols = strips // visits * width
        slab = rows // groups
        vertical, horizontal = tables(rows, width)
        count = vertical.shape[0]
        far = pl.BlockSpec(memory_space=pltpu.HBM)
        coef = jnp.transpose(kernel_coef[0, 0], (1, 0, 2))
        dma = pltpu.SemaphoreType.DMA
        macs = visits * cols * rows * count * (2 * width + 2 * rows)
        return pl.pallas_call(
            functools.partial(kernel, groups, patches),
            out_shape=pltpu.VMEM((1, slab, cols), F32),
            in_specs=[far] * 7,
            out_specs=pl.BlockSpec(memory_space=pltpu.VMEM),

            scratch_shapes=[
                pltpu.SMEM(strip_patch.shape, jnp.int32),
                pltpu.SMEM(strip_slot.shape, jnp.int32),
                pltpu.SMEM(coef.shape, F32),
                pltpu.VMEM((strips, rows, width), BF16),
                pltpu.VMEM((strips, rows, width), BF16),
                pltpu.VMEM(vertical.shape, F32),
                pltpu.VMEM(horizontal.shape, BF16),
                pltpu.VMEM((patches, rows, width), BF16),
                pltpu.VMEM((patches, rows, width), BF16),
                pltpu.VMEM((patches, rows, width), BF16),
                pltpu.VMEM((groups, patches, slab, width), BF16),
                pltpu.VMEM((patches, 1, 128), jnp.int32),
                pltpu.VMEM((groups, patches, 1, 128), jnp.int32),
                pltpu.VMEM((strips * rows, 2 * width), BF16),
                pltpu.VMEM((visits, count * rows, cols), BF16),
                pltpu.VMEM((visits, 2 * rows, count * rows), BF16),
                pltpu.VMEM((visits, rows, cols), F32),
                pltpu.VMEM((visits, rows, cols), BF16),
                pltpu.VMEM((groups, visits, slab, cols), BF16),
                dma((7,)),
            ]
            + [dma] * 12,
            compiler_params=pltpu.CompilerParams(
                collective_id=0, has_side_effects=True, vmem_limit_bytes=48 * 1024 * 1024
            ),
            cost_estimate=pl.CostEstimate(flops=2 * macs, bytes_accessed=1 << 21, transcendentals=0),
        )(
            *[
                pltpu.with_memory_space_constraint(x, pltpu.HBM)
                for x in (
                    strip_patch, strip_slot, coef, strip_image, strip_weight,
                    jnp.asarray(vertical), jnp.asarray(horizontal),
                )
            ]
        )

    return jax.shard_map(
        per_device,
        mesh=mesh,
        in_specs=(
            P("group", "patch", None, None),
            P("group", "patch", None, None),
            P("group", "patch"),
            P("group", "patch"),
            P("group", "patch", None, None, None),
        ),
        out_specs=P("patch", "group", None),
        check_vma=False,
    )
```

```python
import functools

import jax
import jax.numpy as jnp
import ml_dtypes
import numpy as np
from jax import lax
from jax.experimental import pallas as pl
from jax.experimental.pallas import tpu as pltpu
from jax.sharding import PartitionSpec as P

TAPS = 23
HALF = 11
SPREADS = (0.7, 1.5, 3.0)
DEGREES = (4, 3, 2)
MESH = pl.DeviceIdType.MESH
F32 = jnp.float32
BF16 = jnp.bfloat16


def profile_table():
    offsets = np.arange(-HALF, HALF + 1).astype(np.float64)
    profiles = []
    for spread, degree in zip(SPREADS, DEGREES):
        for power in range(degree + 1):
            profile = np.exp(-offsets * offsets / (2.0 * spread * spread)) * (offsets / spread) ** power
            profiles.append(profile / np.sqrt(np.sum(profile * profile)))
    return np.stack(profiles).astype(np.float32).astype(ml_dtypes.bfloat16).astype(np.float32)


def basis_pairs():
    pairs, start = [], 0
    for degree in DEGREES:
        for vertical in range(degree + 1):
            for horizontal in range(degree + 1 - vertical):
                pairs.append((start + vertical, start + horizontal))
        start += degree + 1
    return pairs


def band(profile, inputs, outputs):
    differ = outputs[None, :] - inputs[:, None]
    return np.where(np.abs(differ) <= HALF, profile[np.clip(differ + HALF, 0, 2 * HALF)], 0.0)


def tables(rows, width):
    profiles = profile_table()
    y = np.arange(rows)
    vertical = np.stack([band(p, y, y).T for p in profiles])
    x = np.arange(width)
    halo = np.where(x < width // 2, x + width, x - width)
    lanes = np.concatenate([x, halo])
    horizontal = np.concatenate([band(p, lanes, x) for p in profiles], axis=1)
    return vertical.astype(np.float32), horizontal.astype(ml_dtypes.bfloat16)


def kernel(
    groups, patches,
    patch_hbm, slot_hbm, coef_hbm, img_hbm, wgt_hbm, ver_hbm, hor_hbm, out_ref,
    patch_ref, slot_ref, coef_ref, found,
    img_in, wgt_in, ver, band_h, img_send, img_recv, wgt_send, wgt_recv, lab_send, lab_recv,
    win, hor, mix, mat, mat_send, mat_recv,
    in_sem, lab_ssem, lab_rsem, fwd_ssem, fwd_rsem, img_fsem, img_ssem, img_rsem,
    wgt_ssem, wgt_osem, wgt_rsem, mat_ssem, mat_rsem,
):
    my_group, me = lax.axis_index("group"), lax.axis_index("patch")
    strips, rows, width = img_in.shape
    visits, cols = mat.shape[0], mat.shape[2]
    blocks = strips // visits
    slab = rows // groups
    count = ver.shape[0]
    devices = groups * patches

    loads = [
        pltpu.make_async_copy(src, dst, in_sem.at[i])
        for i, (src, dst) in enumerate(
            [
                (img_hbm.at[0], img_in), (wgt_hbm.at[0], wgt_in), (ver_hbm, ver), (hor_hbm, band_h),
                (patch_hbm, patch_ref), (slot_hbm, slot_ref), (coef_hbm, coef_ref),
            ]
        )
    ]
    for i in (4, 5, 0, 1, 6, 2, 3):
        loads[i].start()

    barrier = pltpu.get_barrier_semaphore()
    mine = my_group * patches + me

    def greet(i, carry):
        other = lax.rem(mine + 1 + i, devices)
        pl.semaphore_signal(
            barrier, inc=1, device_id=(other // patches, lax.rem(other, patches)), device_id_type=MESH
        )
        return carry

    lax.fori_loop(0, devices - 1, greet, 0)

    def find(p, carry):
        source, label = jnp.int32(0), jnp.int32(0)
        for s in range(strips):
            here = patch_ref[0, s] == p
            source = jnp.where(here, s, source)
            label = jnp.where(here, slot_ref[0, s] + 1, label)
        found[0, p] = source
        found[1, p] = label
        return carry

    def pack_label(p, carry):
        lab_send[p] = jnp.full((1, 128), found[1, p], jnp.int32)
        return carry

    def pack_image(p, carry):
        img_send[p] = img_in[found[0, p]]
        return carry

    def pack_weight(p, carry):
        wgt_send[p] = wgt_in[found[0, p]]
        return carry

    def other_patch(i):
        step = lax.select(lax.rem(i, 2) == 0, patches - 1 - lax.div(i, 2), lax.div(i + 1, 2))
        other, bit = jnp.int32(0), 1
        while bit < patches:
            other = other + bit * lax.rem(lax.div(me, bit) + lax.div(step, bit), 2)
            bit *= 2
        return other

    loads[4].wait()
    loads[5].wait()
    lax.fori_loop(0, patches, find, 0)
    loads[0].wait()
    lax.fori_loop(0, patches, pack_image, 0)
    pl.semaphore_wait(barrier, devices - 1)

    def send_label(i, carry):
        p = other_patch(i)
        pltpu.make_async_remote_copy(
            src_ref=lab_send.at[p], dst_ref=lab_recv.at[my_group, me],
            send_sem=lab_ssem, recv_sem=lab_rsem, device_id=(my_group, p), device_id_type=MESH,
        ).start()
        return carry

    def send_image(i, carry, sem=img_ssem):
        p = other_patch(i)
        pltpu.make_async_remote_copy(
            src_ref=img_send.at[p], dst_ref=img_recv.at[me],
            send_sem=sem, recv_sem=img_rsem, device_id=(my_group, p), device_id_type=MESH,
        ).start()
        return carry

    first = patches // 2
    lax.fori_loop(0, first, functools.partial(send_image, sem=img_fsem), 0)
    lax.fori_loop(0, patches, pack_label, 0)
    lax.fori_loop(0, patches - 1, send_label, 0)
    pltpu.make_async_copy(lab_send.at[me], lab_recv.at[my_group, me], lab_rsem).start()
    lax.fori_loop(first, patches - 1, send_image, 0)
    pltpu.make_async_copy(img_send.at[me], img_recv.at[me], img_rsem).start()

    loads[1].wait()
    lax.fori_loop(0, patches, pack_weight, 0)

    loads[2].wait()
    loads[6].wait()
    pairs = basis_pairs()
    down = (2.0 * lax.broadcasted_iota(jnp.int32, (rows, rows), 0).astype(F32) - (rows - 1)) / (rows - 1)

    def mix_visit(v, carry):
        for r in range(count):
            flat = jnp.zeros((rows, rows), F32)
            across = jnp.zeros((rows, rows), F32)
            tilt = jnp.zeros((rows, rows), F32)
            for b, (q, h) in enumerate(pairs):
                if h == r:
                    vertical = ver[q]
                    flat = flat + coef_ref[0, v, b] * vertical
                    across = across + coef_ref[1, v, b] * vertical
                    tilt = tilt + coef_ref[2, v, b] * vertical
            mix[v, :rows, r * rows : (r + 1) * rows] = (flat + down * tilt).astype(BF16)
            mix[v, rows:, r * rows : (r + 1) * rows] = across.astype(BF16)
        return carry

    lax.fori_loop(0, visits, mix_visit, 0)

    pltpu.make_async_copy(img_send.at[pl.ds(0, first)], img_send.at[pl.ds(0, first)], img_fsem).wait()

    def slab_of(g):
        return pl.ds(pl.multiple_of(g * slab, slab), slab)

    def send_weight(i, carry):
        p = other_patch(i)
        for d in range(groups):
            g = lax.rem(my_group + d, groups)
            pltpu.make_async_remote_copy(
                src_ref=wgt_send.at[p, slab_of(g)], dst_ref=wgt_recv.at[my_group, me],
                send_sem=wgt_osem if d == 0 else wgt_ssem, recv_sem=wgt_rsem,
                device_id=(g, p), device_id_type=MESH,
            ).start()
        return carry

    lax.fori_loop(0, patches - 1, send_weight, 0)
    pltpu.make_async_copy(wgt_send.at[me, slab_of(my_group)], wgt_recv.at[my_group, me], wgt_rsem).start()
    for d in range(1, groups):
        g = lax.rem(my_group + d, groups)
        pltpu.make_async_remote_copy(
            src_ref=wgt_send.at[me, slab_of(g)], dst_ref=wgt_recv.at[my_group, me],
            send_sem=wgt_ssem, recv_sem=wgt_rsem, device_id=(g, me), device_id_type=MESH,
        ).start()

    pltpu.make_async_copy(lab_recv.at[0], lab_recv.at[0], lab_rsem).wait()
    for d in range(1, groups):
        pltpu.make_async_remote_copy(
            src_ref=lab_recv.at[my_group], dst_ref=lab_recv.at[my_group],
            send_sem=fwd_ssem, recv_sem=fwd_rsem,
            device_id=(lax.rem(my_group + d, groups), me), device_id_type=MESH,
        ).start()

    def positions(g):
        labels = lab_recv[g]
        order = lax.broadcasted_iota(jnp.int32, labels.shape, 0)
        return [
            jnp.max(jnp.where(labels == t + 1, order, 0)) for t in range(strips)
        ]

    place = positions(my_group)
    pltpu.make_async_copy(img_recv, img_recv, img_rsem).wait()

    zeros = jnp.zeros((rows, width), BF16)
    half = width // 2
    for t in range(strips):
        k = t % blocks
        here = slice(t * rows, (t + 1) * rows)
        win[here, :width] = img_recv[place[t]]
        right = img_recv[place[t + 1]] if k < blocks - 1 else zeros
        left = img_recv[place[t - 1]] if k > 0 else zeros
        win[here, width : width + half] = right[:, :half]
        win[here, width + half :] = left[:, half:]

    loads[3].wait()
    per = 2
    for v in range(visits):
        for j in range(count // per):
            part = jnp.dot(
                win[v * blocks * rows : (v + 1) * blocks * rows, :],
                band_h[:, j * per * width : (j + 1) * per * width],
                preferred_element_type=F32,
            ).astype(BF16)
            for k in range(blocks):
                for i in range(per):
                    r = j * per + i
                    hor[v, r * rows : (r + 1) * rows, k * width : (k + 1) * width] = part[
                        k * rows : (k + 1) * rows, i * width : (i + 1) * width
                    ]

    chunk = 2 * width
    for v in range(visits):
        for c in range(cols // chunk):
            here = slice(c * chunk, (c + 1) * chunk)
            both = jnp.dot(mix[v], hor[v, :, here], preferred_element_type=F32)
            at = lax.broadcasted_iota(jnp.int32, (rows, chunk), 1).astype(F32) + c * chunk
            sideways = (2.0 * at - (cols - 1)) / (cols - 1)
            matched = both[:rows] + sideways * both[rows:]
            mat[v, :, here] = matched
            mat_send[v, :, here] = matched.astype(BF16)
        for d in range(1, groups):
            g = lax.rem(my_group + d, groups)
            pltpu.make_async_remote_copy(
                src_ref=mat_send.at[v, slab_of(g)], dst_ref=mat_recv.at[my_group, v],
                send_sem=mat_ssem, recv_sem=mat_rsem, device_id=(g, me), device_id_type=MESH,
            ).start()

    rest = pl.ds(0, groups - 1)
    pltpu.make_async_copy(lab_recv.at[rest], lab_recv.at[rest], fwd_rsem).wait()
    places = [place]
    for d in range(1, groups):
        places.append(positions(lax.rem(my_group + d, groups)))
    pltpu.make_async_copy(mat_recv.at[rest], mat_recv.at[rest], mat_rsem).wait()
    pltpu.make_async_copy(wgt_recv, wgt_recv, wgt_rsem).wait()

    for k in range(blocks):
        here = slice(k * width, (k + 1) * width)
        numer = jnp.zeros((slab, width), F32)
        denom = jnp.zeros((slab, width), F32)
        for d in range(groups):
            g = lax.rem(my_group + d, groups)
            for v in range(visits):
                weight = wgt_recv[g, places[d][v * blocks + k]].astype(F32)
                if d == 0:
                    matched = mat[v, slab_of(my_group), here]
                else:
                    matched = mat_recv[g, v, :, here].astype(F32)
                numer = numer + weight * matched
                denom = denom + weight
        out_ref[0, :, here] = numer / denom

    some = pl.ds(0, patches - 1)
    last = pl.ds(0, patches - 1 - first)
    pltpu.make_async_copy(img_send.at[last], img_send.at[last], img_ssem).wait()
    pltpu.make_async_copy(lab_send.at[some], lab_send.at[some], lab_ssem).wait()
    pltpu.make_async_copy(lab_recv.at[rest], lab_recv.at[rest], fwd_ssem).wait()
    pltpu.make_async_copy(wgt_recv.at[0, some], wgt_recv.at[0, some], wgt_osem).wait()
    pltpu.make_async_copy(wgt_recv.at[rest], wgt_recv.at[rest], wgt_ssem).wait()
    pltpu.make_async_copy(mat_recv.at[rest], mat_recv.at[rest], mat_ssem).wait()


def solution(mesh):
    groups, patches = mesh.shape["group"], mesh.shape["patch"]

    def per_device(strip_image, strip_weight, strip_patch, strip_slot, kernel_coef):
        _, strips, rows, width = strip_image.shape
        visits = kernel_coef.shape[2]
        cols = strips // visits * width
        slab = rows // groups
        vertical, horizontal = tables(rows, width)
        count = vertical.shape[0]
        far = pl.BlockSpec(memory_space=pltpu.HBM)
        coef = jnp.transpose(kernel_coef[0, 0], (1, 0, 2))
        dma = pltpu.SemaphoreType.DMA
        macs = visits * cols * rows * count * (2 * width + 2 * rows)
        return pl.pallas_call(
            functools.partial(kernel, groups, patches),
            out_shape=pltpu.VMEM((1, slab, cols), F32),
            in_specs=[far] * 7,
            out_specs=pl.BlockSpec(memory_space=pltpu.VMEM),
            scratch_shapes=[
                pltpu.SMEM(strip_patch.shape, jnp.int32),
                pltpu.SMEM(strip_slot.shape, jnp.int32),
                pltpu.SMEM(coef.shape, F32),
                pltpu.SMEM((2, patches), jnp.int32),
                pltpu.VMEM((strips, rows, width), BF16),
                pltpu.VMEM((strips, rows, width), BF16),
                pltpu.VMEM(vertical.shape, F32),
                pltpu.VMEM(horizontal.shape, BF16),
                pltpu.VMEM((patches, rows, width), BF16),
                pltpu.VMEM((patches, rows, width), BF16),
                pltpu.VMEM((patches, rows, width), BF16),
                pltpu.VMEM((groups, patches, slab, width), BF16),
                pltpu.VMEM((patches, 1, 128), jnp.int32),
                pltpu.VMEM((groups, patches, 1, 128), jnp.int32),
                pltpu.VMEM((strips * rows, 2 * width), BF16),
                pltpu.VMEM((visits, count * rows, cols), BF16),
                pltpu.VMEM((visits, 2 * rows, count * rows), BF16),
                pltpu.VMEM((visits, rows, cols), F32),
                pltpu.VMEM((visits, rows, cols), BF16),
                pltpu.VMEM((groups, visits, slab, cols), BF16),
                dma((7,)),
            ]
            + [dma] * 12,
            compiler_params=pltpu.CompilerParams(
                collective_id=0, has_side_effects=True, vmem_limit_bytes=48 * 1024 * 1024
            ),
            cost_estimate=pl.CostEstimate(flops=2 * macs, bytes_accessed=1 << 21, transcendentals=0),
        )(
            *[
                pltpu.with_memory_space_constraint(x, pltpu.HBM)
                for x in (
                    strip_patch, strip_slot, coef, strip_image, strip_weight,
                    jnp.asarray(vertical), jnp.asarray(horizontal),
                )
            ]
        )

    return jax.shard_map(
        per_device,
        mesh=mesh,
        in_specs=(
            P("group", "patch", None, None),
            P("group", "patch", None, None),
            P("group", "patch"),
            P("group", "patch"),
            P("group", "patch", None, None, None),
        ),
        out_specs=P("patch", "group", None),
        check_vma=False,
    )
```

```python
import functools

import jax
import jax.numpy as jnp
import ml_dtypes
import numpy as np
from jax import lax
from jax.experimental import pallas as pl
from jax.experimental.pallas import tpu as pltpu
from jax.sharding import PartitionSpec as P

TAPS = 23
HALF = 11
SPREADS = (0.7, 1.5, 3.0)
DEGREES = (4, 3, 2)
MESH = pl.DeviceIdType.MESH
F32 = jnp.float32
BF16 = jnp.bfloat16


def profile_table():
    offsets = np.arange(-HALF, HALF + 1).astype(np.float64)
    profiles = []
    for spread, degree in zip(SPREADS, DEGREES):
        for power in range(degree + 1):
            profile = np.exp(-offsets * offsets / (2.0 * spread * spread)) * (offsets / spread) ** power
            profiles.append(profile / np.sqrt(np.sum(profile * profile)))
    return np.stack(profiles).astype(np.float32).astype(ml_dtypes.bfloat16).astype(np.float32)


def basis_pairs():
    pairs, start = [], 0
    for degree in DEGREES:
        for vertical in range(degree + 1):
            for horizontal in range(degree + 1 - vertical):
                pairs.append((start + vertical, start + horizontal))
        start += degree + 1
    return pairs


def band(profile, inputs, outputs):
    differ = outputs[None, :] - inputs[:, None]
    return np.where(np.abs(differ) <= HALF, profile[np.clip(differ + HALF, 0, 2 * HALF)], 0.0)


def tables(rows, width):
    profiles = profile_table()
    y = np.arange(rows)
    vertical = np.stack([band(p, y, y).T for p in profiles])
    x = np.arange(width)
    halo = np.where(x < width // 2, x + width, x - width)
    lanes = np.concatenate([x, halo])
    horizontal = np.concatenate([band(p, lanes, x) for p in profiles], axis=1)
    return vertical.astype(np.float32), horizontal.astype(ml_dtypes.bfloat16)


def kernel(
    groups, patches,
    patch_hbm, slot_hbm, coef_hbm, img_hbm, wgt_hbm, ver_hbm, hor_hbm, out_ref,
    patch_ref, slot_ref, coef_ref, found,
    img_in, wgt_in, ver, band_h, img_send, img_recv, wgt_send, wgt_recv, lab_send, lab_recv,
    win, hor, mix, mat, mat_send, mat_recv,
    in_sem, lab_ssem, lab_rsem, fwd_ssem, fwd_rsem, img_fsem, img_ssem, img_rsem,
    wgt_ssem, wgt_osem, wgt_rsem, mat_ssem, mat_rsem,
):
    my_group, me = lax.axis_index("group"), lax.axis_index("patch")
    strips, rows, width = img_in.shape
    visits, cols = mat.shape[0], mat.shape[2]
    blocks = strips // visits
    slab = rows // groups
    count = ver.shape[0]
    devices = groups * patches

    loads = [
        pltpu.make_async_copy(src, dst, in_sem.at[i])
        for i, (src, dst) in enumerate(
            [
                (img_hbm.at[0], img_in), (wgt_hbm.at[0], wgt_in), (ver_hbm, ver), (hor_hbm, band_h),
                (patch_hbm, patch_ref), (slot_hbm, slot_ref), (coef_hbm, coef_ref),
            ]
        )
    ]
    for i in (4, 5, 0, 1, 6, 2, 3):
        loads[i].start()

    barrier = pltpu.get_barrier_semaphore()
    mine = my_group * patches + me

    def greet(i, carry):
        other = lax.rem(mine + 1 + i, devices)
        pl.semaphore_signal(
            barrier, inc=1, device_id=(other // patches, lax.rem(other, patches)), device_id_type=MESH
        )
        return carry

    lax.fori_loop(0, devices - 1, greet, 0)

    def find(p, carry):
        source, label = jnp.int32(0), jnp.int32(0)
        for s in range(strips):
            here = patch_ref[0, s] == p
            source = jnp.where(here, s, source)
            label = jnp.where(here, slot_ref[0, s] + 1, label)
        found[0, p] = source
        found[1, p] = label
        return carry

    def pack_label(p, carry):
        lab_send[p] = jnp.full((1, 128), found[1, p], jnp.int32)
        return carry

    def pack_image(p, carry):
        img_send[p] = img_in[found[0, p]]
        return carry

    def pack_weight(p, carry):
        wgt_send[p] = wgt_in[found[0, p]]
        return carry

    def other_patch(i):
        quarter = patches // 4
        lead = quarter // 2
        j = lax.div(i, 2)
        by_turns = lax.select(
            lax.rem(j - lead + quarter, 2) == 0, quarter + lax.div(j - lead, 2), lead + lax.div(j - lead, 2)
        )
        far = lax.select(j < lead, j, lax.select(j >= quarter + lead, j, by_turns))
        step = lax.select(lax.rem(i, 2) == 0, 2 * quarter + far, j + 1)
        other, bit = jnp.int32(0), 1
        while bit < patches:
            other = other + bit * lax.rem(lax.div(me, bit) + lax.div(step, bit), 2)
            bit *= 2
        return other

    loads[4].wait()
    loads[5].wait()
    lax.fori_loop(0, patches, find, 0)
    loads[0].wait()
    lax.fori_loop(0, patches, pack_image, 0)
    pl.semaphore_wait(barrier, devices - 1)

    def send_label(i, carry):
        p = other_patch(i)
        pltpu.make_async_remote_copy(
            src_ref=lab_send.at[p], dst_ref=lab_recv.at[my_group, me],
            send_sem=lab_ssem, recv_sem=lab_rsem, device_id=(my_group, p), device_id_type=MESH,
        ).start()
        return carry

    def send_image(i, carry, sem=img_ssem):
        p = other_patch(i)
        pltpu.make_async_remote_copy(
            src_ref=img_send.at[p], dst_ref=img_recv.at[me],
            send_sem=sem, recv_sem=img_rsem, device_id=(my_group, p), device_id_type=MESH,
        ).start()
        return carry

    first = patches // 2
    lax.fori_loop(0, first, functools.partial(send_image, sem=img_fsem), 0)
    lax.fori_loop(0, patches, pack_label, 0)
    lax.fori_loop(0, patches - 1, send_label, 0)
    pltpu.make_async_copy(lab_send.at[me], lab_recv.at[my_group, me], lab_rsem).start()
    lax.fori_loop(first, patches - 1, send_image, 0)
    pltpu.make_async_copy(img_send.at[me], img_recv.at[me], img_rsem).start()

    loads[1].wait()
    lax.fori_loop(0, patches, pack_weight, 0)

    loads[2].wait()
    loads[6].wait()
    pairs = basis_pairs()
    down = (2.0 * lax.broadcasted_iota(jnp.int32, (rows, rows), 0).astype(F32) - (rows - 1)) / (rows - 1)

    def mix_visit(v, carry):
        for r in range(count):
            flat = jnp.zeros((rows, rows), F32)
            across = jnp.zeros((rows, rows), F32)
            tilt = jnp.zeros((rows, rows), F32)
            for b, (q, h) in enumerate(pairs):
                if h == r:
                    vertical = ver[q]
                    flat = flat + coef_ref[0, v, b] * vertical
                    across = across + coef_ref[1, v, b] * vertical
                    tilt = tilt + coef_ref[2, v, b] * vertical
            mix[v, :rows, r * rows : (r + 1) * rows] = (flat + down * tilt).astype(BF16)
            mix[v, rows:, r * rows : (r + 1) * rows] = across.astype(BF16)
        return carry

    lax.fori_loop(0, visits, mix_visit, 0)

    pltpu.make_async_copy(img_send.at[pl.ds(0, first)], img_send.at[pl.ds(0, first)], img_fsem).wait()

    def slab_of(g):
        return pl.ds(pl.multiple_of(g * slab, slab), slab)

    def send_weight(i, carry):
        p = other_patch(i)
        for d in range(groups):
            g = lax.rem(my_group + d, groups)
            pltpu.make_async_remote_copy(
                src_ref=wgt_send.at[p, slab_of(g)], dst_ref=wgt_recv.at[my_group, me],
                send_sem=wgt_osem if d == 0 else wgt_ssem, recv_sem=wgt_rsem,
                device_id=(g, p), device_id_type=MESH,
            ).start()
        return carry

    lax.fori_loop(0, patches - 1, send_weight, 0)
    pltpu.make_async_copy(wgt_send.at[me, slab_of(my_group)], wgt_recv.at[my_group, me], wgt_rsem).start()
    for d in range(1, groups):
        g = lax.rem(my_group + d, groups)
        pltpu.make_async_remote_copy(
            src_ref=wgt_send.at[me, slab_of(g)], dst_ref=wgt_recv.at[my_group, me],
            send_sem=wgt_ssem, recv_sem=wgt_rsem, device_id=(g, me), device_id_type=MESH,
        ).start()

    pltpu.make_async_copy(lab_recv.at[0], lab_recv.at[0], lab_rsem).wait()
    for d in range(1, groups):
        pltpu.make_async_remote_copy(
            src_ref=lab_recv.at[my_group], dst_ref=lab_recv.at[my_group],
            send_sem=fwd_ssem, recv_sem=fwd_rsem,
            device_id=(lax.rem(my_group + d, groups), me), device_id_type=MESH,
        ).start()

    def positions(g):
        labels = lab_recv[g]
        order = lax.broadcasted_iota(jnp.int32, labels.shape, 0)
        return [
            jnp.max(jnp.where(labels == t + 1, order, 0)) for t in range(strips)
        ]

    place = positions(my_group)
    pltpu.make_async_copy(img_recv, img_recv, img_rsem).wait()

    zeros = jnp.zeros((rows, width), BF16)
    half = width // 2
    for t in range(strips):
        k = t % blocks
        here = slice(t * rows, (t + 1) * rows)
        win[here, :width] = img_recv[place[t]]
        right = img_recv[place[t + 1]] if k < blocks - 1 else zeros
        left = img_recv[place[t - 1]] if k > 0 else zeros
        win[here, width : width + half] = right[:, :half]
        win[here, width + half :] = left[:, half:]

    loads[3].wait()
    per = 2
    for v in range(visits):
        for j in range(count // per):
            part = jnp.dot(
                win[v * blocks * rows : (v + 1) * blocks * rows, :],
                band_h[:, j * per * width : (j + 1) * per * width],
                preferred_element_type=F32,
            ).astype(BF16)
            for k in range(blocks):
                for i in range(per):
                    r = j * per + i
                    hor[v, r * rows : (r + 1) * rows, k * width : (k + 1) * width] = part[
                        k * rows : (k + 1) * rows, i * width : (i + 1) * width
                    ]

    chunk = 2 * width
    for v in range(visits):
        for c in range(cols // chunk):
            here = slice(c * chunk, (c + 1) * chunk)
            both = jnp.dot(mix[v], hor[v, :, here], preferred_element_type=F32)
            at = lax.broadcasted_iota(jnp.int32, (rows, chunk), 1).astype(F32) + c * chunk
            sideways = (2.0 * at - (cols - 1)) / (cols - 1)
            matched = both[:rows] + sideways * both[rows:]
            mat[v, :, here] = matched
            mat_send[v, :, here] = matched.astype(BF16)
        for d in range(1, groups):
            g = lax.rem(my_group + d, groups)
            pltpu.make_async_remote_copy(
                src_ref=mat_send.at[v, slab_of(g)], dst_ref=mat_recv.at[my_group, v],
                send_sem=mat_ssem, recv_sem=mat_rsem, device_id=(g, me), device_id_type=MESH,
            ).start()

    rest = pl.ds(0, groups - 1)
    pltpu.make_async_copy(lab_recv.at[rest], lab_recv.at[rest], fwd_rsem).wait()
    places = [place]
    for d in range(1, groups):
        places.append(positions(lax.rem(my_group + d, groups)))
    pltpu.make_async_copy(mat_recv.at[rest], mat_recv.at[rest], mat_rsem).wait()
    pltpu.make_async_copy(wgt_recv, wgt_recv, wgt_rsem).wait()

    for k in range(blocks):
        here = slice(k * width, (k + 1) * width)
        numer = jnp.zeros((slab, width), F32)
        denom = jnp.zeros((slab, width), F32)
        for d in range(groups):
            g = lax.rem(my_group + d, groups)
            for v in range(visits):
                weight = wgt_recv[g, places[d][v * blocks + k]].astype(F32)
                if d == 0:
                    matched = mat[v, slab_of(my_group), here]
                else:
                    matched = mat_recv[g, v, :, here].astype(F32)
                numer = numer + weight * matched
                denom = denom + weight
        out_ref[0, :, here] = numer / denom

    some = pl.ds(0, patches - 1)
    last = pl.ds(0, patches - 1 - first)
    pltpu.make_async_copy(img_send.at[last], img_send.at[last], img_ssem).wait()
    pltpu.make_async_copy(lab_send.at[some], lab_send.at[some], lab_ssem).wait()
    pltpu.make_async_copy(lab_recv.at[rest], lab_recv.at[rest], fwd_ssem).wait()
    pltpu.make_async_copy(wgt_recv.at[0, some], wgt_recv.at[0, some], wgt_osem).wait()
    pltpu.make_async_copy(wgt_recv.at[rest], wgt_recv.at[rest], wgt_ssem).wait()
    pltpu.make_async_copy(mat_recv.at[rest], mat_recv.at[rest], mat_ssem).wait()


def solution(mesh):
    groups, patches = mesh.shape["group"], mesh.shape["patch"]

    def per_device(strip_image, strip_weight, strip_patch, strip_slot, kernel_coef):
        _, strips, rows, width = strip_image.shape
        visits = kernel_coef.shape[2]
        cols = strips // visits * width
        slab = rows // groups
        vertical, horizontal = tables(rows, width)
        count = vertical.shape[0]
        far = pl.BlockSpec(memory_space=pltpu.HBM)
        coef = jnp.transpose(kernel_coef[0, 0], (1, 0, 2))
        dma = pltpu.SemaphoreType.DMA
        macs = visits * cols * rows * count * (2 * width + 2 * rows)
        return pl.pallas_call(
            functools.partial(kernel, groups, patches),
            out_shape=pltpu.VMEM((1, slab, cols), F32),
            in_specs=[far] * 7,
            out_specs=pl.BlockSpec(memory_space=pltpu.VMEM),
            scratch_shapes=[
                pltpu.SMEM(strip_patch.shape, jnp.int32),
                pltpu.SMEM(strip_slot.shape, jnp.int32),
                pltpu.SMEM(coef.shape, F32),
                pltpu.SMEM((2, patches), jnp.int32),
                pltpu.VMEM((strips, rows, width), BF16),
                pltpu.VMEM((strips, rows, width), BF16),
                pltpu.VMEM(vertical.shape, F32),
                pltpu.VMEM(horizontal.shape, BF16),
                pltpu.VMEM((patches, rows, width), BF16),
                pltpu.VMEM((patches, rows, width), BF16),
                pltpu.VMEM((patches, rows, width), BF16),
                pltpu.VMEM((groups, patches, slab, width), BF16),
                pltpu.VMEM((patches, 1, 128), jnp.int32),
                pltpu.VMEM((groups, patches, 1, 128), jnp.int32),
                pltpu.VMEM((strips * rows, 2 * width), BF16),
                pltpu.VMEM((visits, count * rows, cols), BF16),
                pltpu.VMEM((visits, 2 * rows, count * rows), BF16),
                pltpu.VMEM((visits, rows, cols), F32),
                pltpu.VMEM((visits, rows, cols), BF16),
                pltpu.VMEM((groups, visits, slab, cols), BF16),
                dma((7,)),
            ]
            + [dma] * 12,
            compiler_params=pltpu.CompilerParams(
                collective_id=0, has_side_effects=True, vmem_limit_bytes=48 * 1024 * 1024
            ),
            cost_estimate=pl.CostEstimate(flops=2 * macs, bytes_accessed=1 << 21, transcendentals=0),
        )(
            *[
                pltpu.with_memory_space_constraint(x, pltpu.HBM)
                for x in (
                    strip_patch, strip_slot, coef, strip_image, strip_weight,
                    jnp.asarray(vertical), jnp.asarray(horizontal),
                )
            ]
        )

    return jax.shard_map(
        per_device,
        mesh=mesh,
        in_specs=(
            P("group", "patch", None, None),
            P("group", "patch", None, None),
            P("group", "patch"),
            P("group", "patch"),
            P("group", "patch", None, None, None),
        ),
        out_specs=P("patch", "group", None),
        check_vma=False,
    )
```

```python
import functools

import jax
import jax.numpy as jnp
import ml_dtypes
import numpy as np
from jax import lax
from jax.experimental import pallas as pl
from jax.experimental.pallas import tpu as pltpu
from jax.sharding import PartitionSpec as P

TAPS = 23
HALF = 11
SPREADS = (0.7, 1.5, 3.0)
DEGREES = (4, 3, 2)
MESH = pl.DeviceIdType.MESH
F32 = jnp.float32
BF16 = jnp.bfloat16


def profile_table():
    offsets = np.arange(-HALF, HALF + 1).astype(np.float64)
    profiles = []
    for spread, degree in zip(SPREADS, DEGREES):
        for power in range(degree + 1):
            profile = np.exp(-offsets * offsets / (2.0 * spread * spread)) * (offsets / spread) ** power
            profiles.append(profile / np.sqrt(np.sum(profile * profile)))
    return np.stack(profiles).astype(np.float32).astype(ml_dtypes.bfloat16).astype(np.float32)


def basis_pairs():
    pairs, start = [], 0
    for degree in DEGREES:
        for vertical in range(degree + 1):
            for horizontal in range(degree + 1 - vertical):
                pairs.append((start + vertical, start + horizontal))
        start += degree + 1
    return pairs


def band(profile, inputs, outputs):
    differ = outputs[None, :] - inputs[:, None]
    return np.where(np.abs(differ) <= HALF, profile[np.clip(differ + HALF, 0, 2 * HALF)], 0.0)


def tables(rows, width):
    profiles = profile_table()
    y = np.arange(rows)
    vertical = np.stack([band(p, y, y).T for p in profiles])
    x = np.arange(width)
    halo = np.where(x < width // 2, x + width, x - width)
    lanes = np.concatenate([x, halo])
    horizontal = np.concatenate([band(p, lanes, x) for p in profiles], axis=1)
    return vertical.astype(np.float32), horizontal.astype(ml_dtypes.bfloat16)


def kernel(
    groups, patches,
    patch_hbm, slot_hbm, coef_hbm, img_hbm, wgt_hbm, ver_hbm, hor_hbm, out_ref,
    patch_ref, slot_ref, coef_ref, found,
    img_in, wgt_in, ver, band_h, img_send, img_recv, wgt_send, wgt_recv, lab_send, lab_recv,
    win, hor, mix, mat, mat_send, mat_recv,
    in_sem, lab_ssem, lab_rsem, fwd_ssem, fwd_rsem, img_fsem, img_ssem, img_rsem,
    wgt_ssem, wgt_osem, wgt_rsem, mat_ssem, mat_rsem,
):
    my_group, me = lax.axis_index("group"), lax.axis_index("patch")
    strips, rows, width = img_in.shape
    visits, cols = mat.shape[0], mat.shape[2]
    blocks = strips // visits
    slab = rows // groups
    count = ver.shape[0]
    devices = groups * patches

    loads = [
        pltpu.make_async_copy(src, dst, in_sem.at[i])
        for i, (src, dst) in enumerate(
            [
                (img_hbm.at[0], img_in), (wgt_hbm.at[0], wgt_in), (ver_hbm, ver), (hor_hbm, band_h),
                (patch_hbm, patch_ref), (slot_hbm, slot_ref), (coef_hbm, coef_ref),
            ]
        )
    ]
    for i in (4, 5, 0, 1, 6, 2, 3):
        loads[i].start()

    barrier = pltpu.get_barrier_semaphore()
    mine = my_group * patches + me

    def greet(i, carry):
        other = lax.rem(mine + 1 + i, devices)
        pl.semaphore_signal(
            barrier, inc=1, device_id=(other // patches, lax.rem(other, patches)), device_id_type=MESH
        )
        return carry

    lax.fori_loop(0, devices - 1, greet, 0)

    def find(p, carry):
        source, label = jnp.int32(0), jnp.int32(0)
        for s in range(strips):
            here = patch_ref[0, s] == p
            source = jnp.where(here, s, source)
            label = jnp.where(here, slot_ref[0, s] + 1, label)
        found[0, p] = source
        found[1, p] = label
        return carry

    def pack_label(p, carry):
        lab_send[p] = jnp.full((1, 128), found[1, p], jnp.int32)
        return carry

    def pack_image(p, carry):
        img_send[p] = img_in[found[0, p]]
        return carry

    def pack_weight(p, carry):
        wgt_send[p] = wgt_in[found[0, p]]
        return carry

    def other_patch(i):
        quarter = patches // 4
        lead = quarter // 2
        j = lax.div(i, 2)
        by_turns = lax.select(
            lax.rem(j - lead + quarter, 2) == 0, quarter + lax.div(j - lead, 2), lead + lax.div(j - lead, 2)
        )
        far = lax.select(j < lead, j, lax.select(j >= quarter + lead, j, by_turns))
        step = lax.select(lax.rem(i, 2) == 0, 2 * quarter + far, j + 1)
        other, bit = jnp.int32(0), 1
        while bit < patches:
            other = other + bit * lax.rem(lax.div(me, bit) + lax.div(step, bit), 2)
            bit *= 2
        return other

    loads[4].wait()
    loads[5].wait()
    lax.fori_loop(0, patches, find, 0)
    loads[0].wait()
    lax.fori_loop(0, patches, pack_image, 0)
    pl.semaphore_wait(barrier, devices - 1)

    def send_label(i, carry):
        p = other_patch(i)
        pltpu.make_async_remote_copy(
            src_ref=lab_send.at[p], dst_ref=lab_recv.at[my_group, me],
            send_sem=lab_ssem, recv_sem=lab_rsem, device_id=(my_group, p), device_id_type=MESH,
        ).start()
        return carry

    def send_image(i, carry, sem=img_ssem):
        p = other_patch(i)
        pltpu.make_async_remote_copy(
            src_ref=img_send.at[p], dst_ref=img_recv.at[me],
            send_sem=sem, recv_sem=img_rsem, device_id=(my_group, p), device_id_type=MESH,
        ).start()
        return carry

    first = patches // 2
    lax.fori_loop(0, first, functools.partial(send_image, sem=img_fsem), 0)
    lax.fori_loop(0, patches, pack_label, 0)
    lax.fori_loop(0, patches - 1, send_label, 0)
    pltpu.make_async_copy(lab_send.at[me], lab_recv.at[my_group, me], lab_rsem).start()
    lax.fori_loop(first, patches - 1, send_image, 0)
    pltpu.make_async_copy(img_send.at[me], img_recv.at[me], img_rsem).start()

    loads[1].wait()
    lax.fori_loop(0, patches, pack_weight, 0)

    loads[2].wait()
    loads[6].wait()
    pairs = basis_pairs()
    down = (2.0 * lax.broadcasted_iota(jnp.int32, (rows, rows), 0).astype(F32) - (rows - 1)) / (rows - 1)

    def mix_visit(v, carry):
        for r in range(count):
            flat = jnp.zeros((rows, rows), F32)
            across = jnp.zeros((rows, rows), F32)
            tilt = jnp.zeros((rows, rows), F32)
            for b, (q, h) in enumerate(pairs):
                if h == r:
                    vertical = ver[q]
                    flat = flat + coef_ref[0, v, b] * vertical
                    across = across + coef_ref[1, v, b] * vertical
                    tilt = tilt + coef_ref[2, v, b] * vertical
            mix[v, :rows, r * rows : (r + 1) * rows] = (flat + down * tilt).astype(BF16)
            mix[v, rows:, r * rows : (r + 1) * rows] = across.astype(BF16)
        return carry

    lax.fori_loop(0, visits, mix_visit, 0)

    pltpu.make_async_copy(img_send.at[pl.ds(0, first)], img_send.at[pl.ds(0, first)], img_fsem).wait()

    def slab_of(g):
        return pl.ds(pl.multiple_of(g * slab, slab), slab)

    def send_weight(i, carry):
        p = other_patch(lax.select(i < first, 2 * i, 2 * (i - first) + 1))
        for d in range(groups):
            g = lax.rem(my_group + d, groups)
            pltpu.make_async_remote_copy(
                src_ref=wgt_send.at[p, slab_of(g)], dst_ref=wgt_recv.at[my_group, me],
                send_sem=wgt_osem if d == 0 else wgt_ssem, recv_sem=wgt_rsem,
                device_id=(g, p), device_id_type=MESH,
            ).start()
        return carry

    lax.fori_loop(0, patches - 1, send_weight, 0)
    pltpu.make_async_copy(wgt_send.at[me, slab_of(my_group)], wgt_recv.at[my_group, me], wgt_rsem).start()
    for d in range(1, groups):
        g = lax.rem(my_group + d, groups)
        pltpu.make_async_remote_copy(
            src_ref=wgt_send.at[me, slab_of(g)], dst_ref=wgt_recv.at[my_group, me],
            send_sem=wgt_ssem, recv_sem=wgt_rsem, device_id=(g, me), device_id_type=MESH,
        ).start()

    pltpu.make_async_copy(lab_recv.at[0], lab_recv.at[0], lab_rsem).wait()
    for d in range(1, groups):
        pltpu.make_async_remote_copy(
            src_ref=lab_recv.at[my_group], dst_ref=lab_recv.at[my_group],
            send_sem=fwd_ssem, recv_sem=fwd_rsem,
            device_id=(lax.rem(my_group + d, groups), me), device_id_type=MESH,
        ).start()

    def positions(g):
        labels = lab_recv[g]
        order = lax.broadcasted_iota(jnp.int32, labels.shape, 0)
        return [
            jnp.max(jnp.where(labels == t + 1, order, 0)) for t in range(strips)
        ]

    place = positions(my_group)
    pltpu.make_async_copy(img_recv, img_recv, img_rsem).wait()

    zeros = jnp.zeros((rows, width), BF16)
    half = width // 2
    for t in range(strips):
        k = t % blocks
        here = slice(t * rows, (t + 1) * rows)
        win[here, :width] = img_recv[place[t]]
        right = img_recv[place[t + 1]] if k < blocks - 1 else zeros
        left = img_recv[place[t - 1]] if k > 0 else zeros
        win[here, width : width + half] = right[:, :half]
        win[here, width + half :] = left[:, half:]

    loads[3].wait()
    per = 2
    for v in range(visits):
        for j in range(count // per):
            part = jnp.dot(
                win[v * blocks * rows : (v + 1) * blocks * rows, :],
                band_h[:, j * per * width : (j + 1) * per * width],
                preferred_element_type=F32,
            ).astype(BF16)
            for k in range(blocks):
                for i in range(per):
                    r = j * per + i
                    hor[v, r * rows : (r + 1) * rows, k * width : (k + 1) * width] = part[
                        k * rows : (k + 1) * rows, i * width : (i + 1) * width
                    ]

    chunk = 2 * width
    for v in range(visits):
        for c in range(cols // chunk):
            here = slice(c * chunk, (c + 1) * chunk)
            both = jnp.dot(mix[v], hor[v, :, here], preferred_element_type=F32)
            at = lax.broadcasted_iota(jnp.int32, (rows, chunk), 1).astype(F32) + c * chunk
            sideways = (2.0 * at - (cols - 1)) / (cols - 1)
            matched = both[:rows] + sideways * both[rows:]
            mat[v, :, here] = matched
            mat_send[v, :, here] = matched.astype(BF16)
        for d in range(1, groups):
            g = lax.rem(my_group + d, groups)
            pltpu.make_async_remote_copy(
                src_ref=mat_send.at[v, slab_of(g)], dst_ref=mat_recv.at[my_group, v],
                send_sem=mat_ssem, recv_sem=mat_rsem, device_id=(g, me), device_id_type=MESH,
            ).start()

    rest = pl.ds(0, groups - 1)
    pltpu.make_async_copy(lab_recv.at[rest], lab_recv.at[rest], fwd_rsem).wait()
    places = [place]
    for d in range(1, groups):
        places.append(positions(lax.rem(my_group + d, groups)))
    pltpu.make_async_copy(mat_recv.at[rest], mat_recv.at[rest], mat_rsem).wait()
    pltpu.make_async_copy(wgt_recv, wgt_recv, wgt_rsem).wait()

    for k in range(blocks):
        here = slice(k * width, (k + 1) * width)
        numer = jnp.zeros((slab, width), F32)
        denom = jnp.zeros((slab, width), F32)
        for d in range(groups):
            g = lax.rem(my_group + d, groups)
            for v in range(visits):
                weight = wgt_recv[g, places[d][v * blocks + k]].astype(F32)
                if d == 0:
                    matched = mat[v, slab_of(my_group), here]
                else:
                    matched = mat_recv[g, v, :, here].astype(F32)
                numer = numer + weight * matched
                denom = denom + weight
        out_ref[0, :, here] = numer / denom

    some = pl.ds(0, patches - 1)
    last = pl.ds(0, patches - 1 - first)
    pltpu.make_async_copy(img_send.at[last], img_send.at[last], img_ssem).wait()
    pltpu.make_async_copy(lab_send.at[some], lab_send.at[some], lab_ssem).wait()
    pltpu.make_async_copy(lab_recv.at[rest], lab_recv.at[rest], fwd_ssem).wait()
    pltpu.make_async_copy(wgt_recv.at[0, some], wgt_recv.at[0, some], wgt_osem).wait()
    pltpu.make_async_copy(wgt_recv.at[rest], wgt_recv.at[rest], wgt_ssem).wait()
    pltpu.make_async_copy(mat_recv.at[rest], mat_recv.at[rest], mat_ssem).wait()


def solution(mesh):
    groups, patches = mesh.shape["group"], mesh.shape["patch"]

    def per_device(strip_image, strip_weight, strip_patch, strip_slot, kernel_coef):
        _, strips, rows, width = strip_image.shape
        visits = kernel_coef.shape[2]
        cols = strips // visits * width
        slab = rows // groups
        vertical, horizontal = tables(rows, width)
        count = vertical.shape[0]
        far = pl.BlockSpec(memory_space=pltpu.HBM)
        coef = jnp.transpose(kernel_coef[0, 0], (1, 0, 2))
        dma = pltpu.SemaphoreType.DMA
        macs = visits * cols * rows * count * (2 * width + 2 * rows)
        return pl.pallas_call(
            functools.partial(kernel, groups, patches),
            out_shape=pltpu.VMEM((1, slab, cols), F32),
            in_specs=[far] * 7,
            out_specs=pl.BlockSpec(memory_space=pltpu.VMEM),
            scratch_shapes=[
                pltpu.SMEM(strip_patch.shape, jnp.int32),
                pltpu.SMEM(strip_slot.shape, jnp.int32),
                pltpu.SMEM(coef.shape, F32),
                pltpu.SMEM((2, patches), jnp.int32),
                pltpu.VMEM((strips, rows, width), BF16),
                pltpu.VMEM((strips, rows, width), BF16),
                pltpu.VMEM(vertical.shape, F32),
                pltpu.VMEM(horizontal.shape, BF16),
                pltpu.VMEM((patches, rows, width), BF16),
                pltpu.VMEM((patches, rows, width), BF16),
                pltpu.VMEM((patches, rows, width), BF16),
                pltpu.VMEM((groups, patches, slab, width), BF16),
                pltpu.VMEM((patches, 1, 128), jnp.int32),
                pltpu.VMEM((groups, patches, 1, 128), jnp.int32),
                pltpu.VMEM((strips * rows, 2 * width), BF16),
                pltpu.VMEM((visits, count * rows, cols), BF16),
                pltpu.VMEM((visits, 2 * rows, count * rows), BF16),
                pltpu.VMEM((visits, rows, cols), F32),
                pltpu.VMEM((visits, rows, cols), BF16),
                pltpu.VMEM((groups, visits, slab, cols), BF16),
                dma((7,)),
            ]
            + [dma] * 12,
            compiler_params=pltpu.CompilerParams(
                collective_id=0, has_side_effects=True, vmem_limit_bytes=48 * 1024 * 1024
            ),
            cost_estimate=pl.CostEstimate(flops=2 * macs, bytes_accessed=1 << 21, transcendentals=0),
        )(
            *[
                pltpu.with_memory_space_constraint(x, pltpu.HBM)
                for x in (
                    strip_patch, strip_slot, coef, strip_image, strip_weight,
                    jnp.asarray(vertical), jnp.asarray(horizontal),
                )
            ]
        )

    return jax.shard_map(
        per_device,
        mesh=mesh,
        in_specs=(
            P("group", "patch", None, None),
            P("group", "patch", None, None),
            P("group", "patch"),
            P("group", "patch"),
            P("group", "patch", None, None, None),
        ),
        out_specs=P("patch", "group", None),
        check_vma=False,
    )
```

```python
import functools

import jax
import jax.numpy as jnp
import ml_dtypes
import numpy as np
from jax import lax
from jax.experimental import pallas as pl
from jax.experimental.pallas import tpu as pltpu
from jax.sharding import PartitionSpec as P

TAPS = 23
HALF = 11
SPREADS = (0.7, 1.5, 3.0)
DEGREES = (4, 3, 2)
MESH = pl.DeviceIdType.MESH
F32 = jnp.float32
BF16 = jnp.bfloat16


def profile_table():
    offsets = np.arange(-HALF, HALF + 1).astype(np.float64)
    profiles = []
    for spread, degree in zip(SPREADS, DEGREES):
        for power in range(degree + 1):
            profile = np.exp(-offsets * offsets / (2.0 * spread * spread)) * (offsets / spread) ** power
            profiles.append(profile / np.sqrt(np.sum(profile * profile)))
    return np.stack(profiles).astype(np.float32).astype(ml_dtypes.bfloat16).astype(np.float32)


def basis_pairs():
    pairs, start = [], 0
    for degree in DEGREES:
        for vertical in range(degree + 1):
            for horizontal in range(degree + 1 - vertical):
                pairs.append((start + vertical, start + horizontal))
        start += degree + 1
    return pairs


def band(profile, inputs, outputs):
    differ = outputs[None, :] - inputs[:, None]
    return np.where(np.abs(differ) <= HALF, profile[np.clip(differ + HALF, 0, 2 * HALF)], 0.0)


def tables(rows, width):
    profiles = profile_table()
    y = np.arange(rows)
    vertical = np.stack([band(p, y, y).T for p in profiles])
    x = np.arange(width)
    halo = np.where(x < width // 2, x + width, x - width)
    lanes = np.concatenate([x, halo])
    horizontal = np.concatenate([band(p, lanes, x) for p in profiles], axis=1)
    return vertical.astype(np.float32), horizontal.astype(ml_dtypes.bfloat16)


def kernel(
    groups, patches,
    patch_hbm, slot_hbm, coef_hbm, img_hbm, wgt_hbm, ver_hbm, hor_hbm, out_ref,
    patch_ref, slot_ref, coef_ref, found,
    img_in, wgt_in, ver, band_h, img_send, img_recv, wgt_send, wgt_recv, lab_send, lab_recv,
    win, hor, mix, mat, mat_send, mat_recv,
    in_sem, lab_ssem, lab_rsem, fwd_ssem, fwd_rsem, img_fsem, img_ssem, img_rsem,
    wgt_ssem, wgt_osem, wgt_rsem, mat_ssem, mat_rsem,
):
    my_group, me = lax.axis_index("group"), lax.axis_index("patch")
    strips, rows, width = img_in.shape
    visits, cols = mat.shape[0], mat.shape[2]
    blocks = strips // visits
    slab = rows // groups
    count = ver.shape[0]
    devices = groups * patches

    loads = [
        pltpu.make_async_copy(src, dst, in_sem.at[i])
        for i, (src, dst) in enumerate(
            [
                (img_hbm.at[0], img_in), (wgt_hbm.at[0], wgt_in), (ver_hbm, ver), (hor_hbm, band_h),
                (patch_hbm, patch_ref), (slot_hbm, slot_ref), (coef_hbm, coef_ref),
            ]
        )
    ]
    for i in (4, 5, 0, 1, 6, 2, 3):
        loads[i].start()

    barrier = pltpu.get_barrier_semaphore()
    mine = my_group * patches + me

    def greet(i, carry):
        other = lax.rem(mine + 1 + i, devices)
        pl.semaphore_signal(
            barrier, inc=1, device_id=(other // patches, lax.rem(other, patches)), device_id_type=MESH
        )
        return carry

    lax.fori_loop(0, devices - 1, greet, 0)

    def find(p, carry):
        source, label = jnp.int32(0), jnp.int32(0)
        for s in range(strips):
            here = patch_ref[0, s] == p
            source = jnp.where(here, s, source)
            label = jnp.where(here, slot_ref[0, s] + 1, label)
        found[0, p] = source
        found[1, p] = label
        return carry

    def pack_label(p, carry):
        lab_send[p] = jnp.full((1, 128), found[1, p], jnp.int32)
        return carry

    def pack_image(p, carry):
        img_send[p] = img_in[found[0, p]]
        return carry

    def pack_weight(p, carry):
        wgt_send[p] = wgt_in[found[0, p]]
        return carry

    def other_patch(i):
        quarter = patches // 4
        lead = quarter // 2
        j = lax.div(i, 2)
        by_turns = lax.select(
            lax.rem(j - lead + quarter, 2) == 0, quarter + lax.div(j - lead, 2), lead + lax.div(j - lead, 2)
        )
        far = lax.select(j < lead, j, lax.select(j >= quarter + lead, j, by_turns))
        step = lax.select(lax.rem(i, 2) == 0, 2 * quarter + far, j + 1)
        other, bit = jnp.int32(0), 1
        while bit < patches:
            other = other + bit * lax.rem(lax.div(me, bit) + lax.div(step, bit), 2)
            bit *= 2
        return other

    loads[4].wait()
    loads[5].wait()
    lax.fori_loop(0, patches, find, 0)
    loads[0].wait()
    lax.fori_loop(0, patches, pack_image, 0)
    pl.semaphore_wait(barrier, devices - 1)

    def send_label(i, carry):
        p = other_patch(i)
        pltpu.make_async_remote_copy(
            src_ref=lab_send.at[p], dst_ref=lab_recv.at[my_group, me],
            send_sem=lab_ssem, recv_sem=lab_rsem, device_id=(my_group, p), device_id_type=MESH,
        ).start()
        return carry

    def send_image(i, carry, sem=img_ssem):
        p = other_patch(i)
        pltpu.make_async_remote_copy(
            src_ref=img_send.at[p], dst_ref=img_recv.at[me],
            send_sem=sem, recv_sem=img_rsem, device_id=(my_group, p), device_id_type=MESH,
        ).start()
        return carry

    first = patches // 2
    lax.fori_loop(0, first, functools.partial(send_image, sem=img_fsem), 0)
    lax.fori_loop(0, patches, pack_label, 0)
    lax.fori_loop(0, patches - 1, send_label, 0)
    pltpu.make_async_copy(lab_send.at[me], lab_recv.at[my_group, me], lab_rsem).start()
    lax.fori_loop(first, patches - 1, send_image, 0)
    pltpu.make_async_copy(img_send.at[me], img_recv.at[me], img_rsem).start()

    loads[1].wait()
    lax.fori_loop(0, patches, pack_weight, 0)

    loads[2].wait()
    loads[6].wait()
    pairs = basis_pairs()
    down = (2.0 * lax.broadcasted_iota(jnp.int32, (rows, rows), 0).astype(F32) - (rows - 1)) / (rows - 1)

    def mix_visit(v, carry):
        for r in range(count):
            flat = jnp.zeros((rows, rows), F32)
            across = jnp.zeros((rows, rows), F32)
            tilt = jnp.zeros((rows, rows), F32)
            for b, (q, h) in enumerate(pairs):
                if h == r:
                    vertical = ver[q]
                    flat = flat + coef_ref[0, v, b] * vertical
                    across = across + coef_ref[1, v, b] * vertical
                    tilt = tilt + coef_ref[2, v, b] * vertical
            mix[v, :rows, r * rows : (r + 1) * rows] = (flat + down * tilt).astype(BF16)
            mix[v, rows:, r * rows : (r + 1) * rows] = across.astype(BF16)
        return carry

    lax.fori_loop(0, visits, mix_visit, 0)

    pltpu.make_async_copy(img_send.at[pl.ds(0, first)], img_send.at[pl.ds(0, first)], img_fsem).wait()

    def slab_of(g):
        return pl.ds(pl.multiple_of(g * slab, slab), slab)

    def send_weight(i, carry):
        near = first - 1
        p = other_patch(lax.select(i < near, 2 * i + 1, 2 * (i - near)))
        for d in range(groups):
            g = lax.rem(my_group + d, groups)
            pltpu.make_async_remote_copy(
                src_ref=wgt_send.at[p, slab_of(g)], dst_ref=wgt_recv.at[my_group, me],
                send_sem=wgt_osem if d == 0 else wgt_ssem, recv_sem=wgt_rsem,
                device_id=(g, p), device_id_type=MESH,
            ).start()
        return carry

    lax.fori_loop(0, patches - 1, send_weight, 0)
    pltpu.make_async_copy(wgt_send.at[me, slab_of(my_group)], wgt_recv.at[my_group, me], wgt_rsem).start()
    for d in range(1, groups):
        g = lax.rem(my_group + d, groups)
        pltpu.make_async_remote_copy(
            src_ref=wgt_send.at[me, slab_of(g)], dst_ref=wgt_recv.at[my_group, me],
            send_sem=wgt_ssem, recv_sem=wgt_rsem, device_id=(g, me), device_id_type=MESH,
        ).start()

    pltpu.make_async_copy(lab_recv.at[0], lab_recv.at[0], lab_rsem).wait()
    for d in range(1, groups):
        pltpu.make_async_remote_copy(
            src_ref=lab_recv.at[my_group], dst_ref=lab_recv.at[my_group],
            send_sem=fwd_ssem, recv_sem=fwd_rsem,
            device_id=(lax.rem(my_group + d, groups), me), device_id_type=MESH,
        ).start()

    def positions(g):
        labels = lab_recv[g]
        order = lax.broadcasted_iota(jnp.int32, labels.shape, 0)
        return [
            jnp.max(jnp.where(labels == t + 1, order, 0)) for t in range(strips)
        ]

    place = positions(my_group)
    pltpu.make_async_copy(img_recv, img_recv, img_rsem).wait()

    zeros = jnp.zeros((rows, width), BF16)
    half = width // 2
    for t in range(strips):
        k = t % blocks
        here = slice(t * rows, (t + 1) * rows)
        win[here, :width] = img_recv[place[t]]
        right = img_recv[place[t + 1]] if k < blocks - 1 else zeros
        left = img_recv[place[t - 1]] if k > 0 else zeros
        win[here, width : width + half] = right[:, :half]
        win[here, width + half :] = left[:, half:]

    loads[3].wait()
    per = 2
    for v in range(visits):
        for j in range(count // per):
            part = jnp.dot(
                win[v * blocks * rows : (v + 1) * blocks * rows, :],
                band_h[:, j * per * width : (j + 1) * per * width],
                preferred_element_type=F32,
            ).astype(BF16)
            for k in range(blocks):
                for i in range(per):
                    r = j * per + i
                    hor[v, r * rows : (r + 1) * rows, k * width : (k + 1) * width] = part[
                        k * rows : (k + 1) * rows, i * width : (i + 1) * width
                    ]

    chunk = 2 * width
    for v in range(visits):
        for c in range(cols // chunk):
            here = slice(c * chunk, (c + 1) * chunk)
            both = jnp.dot(mix[v], hor[v, :, here], preferred_element_type=F32)
            at = lax.broadcasted_iota(jnp.int32, (rows, chunk), 1).astype(F32) + c * chunk
            sideways = (2.0 * at - (cols - 1)) / (cols - 1)
            matched = both[:rows] + sideways * both[rows:]
            mat[v, :, here] = matched
            mat_send[v, :, here] = matched.astype(BF16)
        for d in range(1, groups):
            g = lax.rem(my_group + d, groups)
            pltpu.make_async_remote_copy(
                src_ref=mat_send.at[v, slab_of(g)], dst_ref=mat_recv.at[my_group, v],
                send_sem=mat_ssem, recv_sem=mat_rsem, device_id=(g, me), device_id_type=MESH,
            ).start()

    rest = pl.ds(0, groups - 1)
    pltpu.make_async_copy(lab_recv.at[rest], lab_recv.at[rest], fwd_rsem).wait()
    places = [place]
    for d in range(1, groups):
        places.append(positions(lax.rem(my_group + d, groups)))
    pltpu.make_async_copy(mat_recv.at[rest], mat_recv.at[rest], mat_rsem).wait()
    pltpu.make_async_copy(wgt_recv, wgt_recv, wgt_rsem).wait()

    for k in range(blocks):
        here = slice(k * width, (k + 1) * width)
        numer = jnp.zeros((slab, width), F32)
        denom = jnp.zeros((slab, width), F32)
        for d in range(groups):
            g = lax.rem(my_group + d, groups)
            for v in range(visits):
                weight = wgt_recv[g, places[d][v * blocks + k]].astype(F32)
                if d == 0:
                    matched = mat[v, slab_of(my_group), here]
                else:
                    matched = mat_recv[g, v, :, here].astype(F32)
                numer = numer + weight * matched
                denom = denom + weight
        out_ref[0, :, here] = numer / denom

    some = pl.ds(0, patches - 1)
    last = pl.ds(0, patches - 1 - first)
    pltpu.make_async_copy(img_send.at[last], img_send.at[last], img_ssem).wait()
    pltpu.make_async_copy(lab_send.at[some], lab_send.at[some], lab_ssem).wait()
    pltpu.make_async_copy(lab_recv.at[rest], lab_recv.at[rest], fwd_ssem).wait()
    pltpu.make_async_copy(wgt_recv.at[0, some], wgt_recv.at[0, some], wgt_osem).wait()
    pltpu.make_async_copy(wgt_recv.at[rest], wgt_recv.at[rest], wgt_ssem).wait()
    pltpu.make_async_copy(mat_recv.at[rest], mat_recv.at[rest], mat_ssem).wait()


def solution(mesh):
    groups, patches = mesh.shape["group"], mesh.shape["patch"]

    def per_device(strip_image, strip_weight, strip_patch, strip_slot, kernel_coef):
        _, strips, rows, width = strip_image.shape
        visits = kernel_coef.shape[2]
        cols = strips // visits * width
        slab = rows // groups
        vertical, horizontal = tables(rows, width)
        count = vertical.shape[0]
        far = pl.BlockSpec(memory_space=pltpu.HBM)
        coef = jnp.transpose(kernel_coef[0, 0], (1, 0, 2))
        dma = pltpu.SemaphoreType.DMA
        macs = visits * cols * rows * count * (2 * width + 2 * rows)
        return pl.pallas_call(
            functools.partial(kernel, groups, patches),
            out_shape=pltpu.VMEM((1, slab, cols), F32),
            in_specs=[far] * 7,
            out_specs=pl.BlockSpec(memory_space=pltpu.VMEM),
            scratch_shapes=[
                pltpu.SMEM(strip_patch.shape, jnp.int32),
                pltpu.SMEM(strip_slot.shape, jnp.int32),
                pltpu.SMEM(coef.shape, F32),
                pltpu.SMEM((2, patches), jnp.int32),
                pltpu.VMEM((strips, rows, width), BF16),
                pltpu.VMEM((strips, rows, width), BF16),
                pltpu.VMEM(vertical.shape, F32),
                pltpu.VMEM(horizontal.shape, BF16),
                pltpu.VMEM((patches, rows, width), BF16),
                pltpu.VMEM((patches, rows, width), BF16),
                pltpu.VMEM((patches, rows, width), BF16),
                pltpu.VMEM((groups, patches, slab, width), BF16),
                pltpu.VMEM((patches, 1, 128), jnp.int32),
                pltpu.VMEM((groups, patches, 1, 128), jnp.int32),
                pltpu.VMEM((strips * rows, 2 * width), BF16),
                pltpu.VMEM((visits, count * rows, cols), BF16),
                pltpu.VMEM((visits, 2 * rows, count * rows), BF16),
                pltpu.VMEM((visits, rows, cols), F32),
                pltpu.VMEM((visits, rows, cols), BF16),
                pltpu.VMEM((groups, visits, slab, cols), BF16),
                dma((7,)),
            ]
            + [dma] * 12,
            compiler_params=pltpu.CompilerParams(
                collective_id=0, has_side_effects=True, vmem_limit_bytes=48 * 1024 * 1024
            ),
            cost_estimate=pl.CostEstimate(flops=2 * macs, bytes_accessed=1 << 21, transcendentals=0),
        )(
            *[
                pltpu.with_memory_space_constraint(x, pltpu.HBM)
                for x in (
                    strip_patch, strip_slot, coef, strip_image, strip_weight,
                    jnp.asarray(vertical), jnp.asarray(horizontal),
                )
            ]
        )

    return jax.shard_map(
        per_device,
        mesh=mesh,
        in_specs=(
            P("group", "patch", None, None),
            P("group", "patch", None, None),
            P("group", "patch"),
            P("group", "patch"),
            P("group", "patch", None, None, None),
        ),
        out_specs=P("patch", "group", None),
        check_vma=False,
    )
```

```python
import functools

import jax
import jax.numpy as jnp
import ml_dtypes
import numpy as np
from jax import lax
from jax.experimental import pallas as pl
from jax.experimental.pallas import tpu as pltpu
from jax.sharding import PartitionSpec as P

TAPS = 23
HALF = 11
SPREADS = (0.7, 1.5, 3.0)
DEGREES = (4, 3, 2)
MESH = pl.DeviceIdType.MESH
F32 = jnp.float32
BF16 = jnp.bfloat16


def profile_table():
    offsets = np.arange(-HALF, HALF + 1).astype(np.float64)
    profiles = []
    for spread, degree in zip(SPREADS, DEGREES):
        for power in range(degree + 1):
            profile = np.exp(-offsets * offsets / (2.0 * spread * spread)) * (offsets / spread) ** power
            profiles.append(profile / np.sqrt(np.sum(profile * profile)))
    return np.stack(profiles).astype(np.float32).astype(ml_dtypes.bfloat16).astype(np.float32)


def basis_pairs():
    pairs, start = [], 0
    for degree in DEGREES:
        for vertical in range(degree + 1):
            for horizontal in range(degree + 1 - vertical):
                pairs.append((start + vertical, start + horizontal))
        start += degree + 1
    return pairs


def band(profile, inputs, outputs):
    differ = outputs[None, :] - inputs[:, None]
    return np.where(np.abs(differ) <= HALF, profile[np.clip(differ + HALF, 0, 2 * HALF)], 0.0)


def tables(rows, width):
    profiles = profile_table()
    y = np.arange(rows)
    vertical = np.stack([band(p, y, y).T for p in profiles])
    x = np.arange(width)
    halo = np.where(x < width // 2, x + width, x - width)
    lanes = np.concatenate([x, halo])
    horizontal = np.concatenate([band(p, lanes, x) for p in profiles], axis=1)
    return vertical.astype(np.float32), horizontal.astype(ml_dtypes.bfloat16)


def kernel(
    groups, patches,
    patch_hbm, slot_hbm, coef_hbm, img_hbm, wgt_hbm, ver_hbm, hor_hbm, out_ref,
    patch_ref, slot_ref, coef_ref, found,
    img_in, wgt_in, ver, band_h, img_send, img_recv, wgt_send, wgt_recv, lab_send, lab_recv,
    win, hor, mix, mat, mat_send, mat_recv,
    in_sem, lab_ssem, lab_rsem, fwd_ssem, fwd_rsem, img_fsem, img_ssem, img_rsem,
    wgt_ssem, wgt_osem, wgt_rsem, mat_ssem, mat_rsem,
):
    my_group, me = lax.axis_index("group"), lax.axis_index("patch")
    strips, rows, width = img_in.shape
    visits, cols = mat.shape[0], mat.shape[2]
    blocks = strips // visits
    slab = rows // groups
    count = ver.shape[0]
    devices = groups * patches

    loads = [
        pltpu.make_async_copy(src, dst, in_sem.at[i])
        for i, (src, dst) in enumerate(
            [
                (img_hbm.at[0], img_in), (wgt_hbm.at[0], wgt_in), (ver_hbm, ver), (hor_hbm, band_h),
                (patch_hbm, patch_ref), (slot_hbm, slot_ref), (coef_hbm, coef_ref),
            ]
        )
    ]
    for i in (4, 5, 0, 1, 6, 2, 3):
        loads[i].start()

    barrier = pltpu.get_barrier_semaphore()
    mine = my_group * patches + me

    def greet(i, carry):
        other = lax.rem(mine + 1 + i, devices)
        pl.semaphore_signal(
            barrier, inc=1, device_id=(other // patches, lax.rem(other, patches)), device_id_type=MESH
        )
        return carry

    lax.fori_loop(0, devices - 1, greet, 0)

    def find(p, carry):
        source, label = jnp.int32(0), jnp.int32(0)
        for s in range(strips):
            here = patch_ref[0, s] == p
            source = jnp.where(here, s, source)
            label = jnp.where(here, slot_ref[0, s] + 1, label)
        found[0, p] = source
        found[1, p] = label
        return carry

    def pack_label(p, carry):
        lab_send[p] = jnp.full((1, 128), found[1, p], jnp.int32)
        return carry

    def pack_image(p, carry):
        img_send[p] = img_in[found[0, p]]
        return carry

    def pack_weight(p, carry):
        wgt_send[p] = wgt_in[found[0, p]]
        return carry

    def other_patch(i):
        quarter = patches // 4
        lead = quarter - quarter // 4
        j = lax.div(i, 2)
        by_turns = lax.select(
            lax.rem(j - lead + quarter, 2) == 0, quarter + lax.div(j - lead, 2), lead + lax.div(j - lead, 2)
        )
        far = lax.select(j < lead, j, lax.select(j >= 2 * quarter - lead, j, by_turns))
        step = lax.select(lax.rem(i, 2) == 0, 2 * quarter + far, j + 1)
        other, bit = jnp.int32(0), 1
        while bit < patches:
            other = other + bit * lax.rem(lax.div(me, bit) + lax.div(step, bit), 2)
            bit *= 2
        return other

    loads[4].wait()
    loads[5].wait()
    lax.fori_loop(0, patches, find, 0)
    loads[0].wait()
    lax.fori_loop(0, patches, pack_image, 0)
    pl.semaphore_wait(barrier, devices - 1)

    def send_label(i, carry):
        p = other_patch(i)
        pltpu.make_async_remote_copy(
            src_ref=lab_send.at[p], dst_ref=lab_recv.at[my_group, me],
            send_sem=lab_ssem, recv_sem=lab_rsem, device_id=(my_group, p), device_id_type=MESH,
        ).start()
        return carry

    def send_image(i, carry, sem=img_ssem):
        p = other_patch(lax.select(i < patches // 2, 2 * i, 2 * (i - patches // 2) + 1))
        pltpu.make_async_remote_copy(
            src_ref=img_send.at[p], dst_ref=img_recv.at[me],
            send_sem=sem, recv_sem=img_rsem, device_id=(my_group, p), device_id_type=MESH,
        ).start()
        return carry

    first = patches // 4
    lax.fori_loop(0, first, functools.partial(send_image, sem=img_fsem), 0)
    lax.fori_loop(first, 2 * first, send_image, 0)
    lax.fori_loop(0, patches, pack_label, 0)
    lax.fori_loop(0, patches - 1, send_label, 0)
    pltpu.make_async_copy(lab_send.at[me], lab_recv.at[my_group, me], lab_rsem).start()
    lax.fori_loop(2 * first, patches - 1, send_image, 0)
    pltpu.make_async_copy(img_send.at[me], img_recv.at[me], img_rsem).start()

    loads[1].wait()
    lax.fori_loop(0, patches, pack_weight, 0)

    loads[2].wait()
    loads[6].wait()
    pairs = basis_pairs()
    down = (2.0 * lax.broadcasted_iota(jnp.int32, (rows, rows), 0).astype(F32) - (rows - 1)) / (rows - 1)

    def mix_visit(v, carry):
        for r in range(count):
            flat = jnp.zeros((rows, rows), F32)
            across = jnp.zeros((rows, rows), F32)
            tilt = jnp.zeros((rows, rows), F32)
            for b, (q, h) in enumerate(pairs):
                if h == r:
                    vertical = ver[q]
                    flat = flat + coef_ref[0, v, b] * vertical
                    across = across + coef_ref[1, v, b] * vertical
                    tilt = tilt + coef_ref[2, v, b] * vertical
            mix[v, :rows, r * rows : (r + 1) * rows] = (flat + down * tilt).astype(BF16)
            mix[v, rows:, r * rows : (r + 1) * rows] = across.astype(BF16)
        return carry

    lax.fori_loop(0, visits, mix_visit, 0)

    pltpu.make_async_copy(img_send.at[pl.ds(0, first)], img_send.at[pl.ds(0, first)], img_fsem).wait()

    def slab_of(g):
        return pl.ds(pl.multiple_of(g * slab, slab), slab)

    def send_weight(i, carry):
        near = patches // 2 - 1
        p = other_patch(lax.select(i < near, 2 * i + 1, 2 * (i - near)))
        for d in range(groups):
            g = lax.rem(my_group + d, groups)
            pltpu.make_async_remote_copy(
                src_ref=wgt_send.at[p, slab_of(g)], dst_ref=wgt_recv.at[my_group, me],
                send_sem=wgt_osem if d == 0 else wgt_ssem, recv_sem=wgt_rsem,
                device_id=(g, p), device_id_type=MESH,
            ).start()
        return carry

    lax.fori_loop(0, patches - 1, send_weight, 0)
    pltpu.make_async_copy(wgt_send.at[me, slab_of(my_group)], wgt_recv.at[my_group, me], wgt_rsem).start()
    for d in range(1, groups):
        g = lax.rem(my_group + d, groups)
        pltpu.make_async_remote_copy(
            src_ref=wgt_send.at[me, slab_of(g)], dst_ref=wgt_recv.at[my_group, me],
            send_sem=wgt_ssem, recv_sem=wgt_rsem, device_id=(g, me), device_id_type=MESH,
        ).start()

    pltpu.make_async_copy(lab_recv.at[0], lab_recv.at[0], lab_rsem).wait()
    for d in range(1, groups):
        pltpu.make_async_remote_copy(
            src_ref=lab_recv.at[my_group], dst_ref=lab_recv.at[my_group],
            send_sem=fwd_ssem, recv_sem=fwd_rsem,
            device_id=(lax.rem(my_group + d, groups), me), device_id_type=MESH,
        ).start()

    def positions(g):
        labels = lab_recv[g]
        order = lax.broadcasted_iota(jnp.int32, labels.shape, 0)
        return [
            jnp.max(jnp.where(labels == t + 1, order, 0)) for t in range(strips)
        ]

    place = positions(my_group)
    pltpu.make_async_copy(img_recv, img_recv, img_rsem).wait()

    zeros = jnp.zeros((rows, width), BF16)
    half = width // 2
    for t in range(strips):
        k = t % blocks
        here = slice(t * rows, (t + 1) * rows)
        win[here, :width] = img_recv[place[t]]
        right = img_recv[place[t + 1]] if k < blocks - 1 else zeros
        left = img_recv[place[t - 1]] if k > 0 else zeros
        win[here, width : width + half] = right[:, :half]
        win[here, width + half :] = left[:, half:]

    loads[3].wait()
    per = 2
    for v in range(visits):
        for j in range(count // per):
            part = jnp.dot(
                win[v * blocks * rows : (v + 1) * blocks * rows, :],
                band_h[:, j * per * width : (j + 1) * per * width],
                preferred_element_type=F32,
            ).astype(BF16)
            for k in range(blocks):
                for i in range(per):
                    r = j * per + i
                    hor[v, r * rows : (r + 1) * rows, k * width : (k + 1) * width] = part[
                        k * rows : (k + 1) * rows, i * width : (i + 1) * width
                    ]

    chunk = 2 * width
    for v in range(visits):
        for c in range(cols // chunk):
            here = slice(c * chunk, (c + 1) * chunk)
            both = jnp.dot(mix[v], hor[v, :, here], preferred_element_type=F32)
            at = lax.broadcasted_iota(jnp.int32, (rows, chunk), 1).astype(F32) + c * chunk
            sideways = (2.0 * at - (cols - 1)) / (cols - 1)
            matched = both[:rows] + sideways * both[rows:]
            mat[v, :, here] = matched
            mat_send[v, :, here] = matched.astype(BF16)
        for d in range(1, groups):
            g = lax.rem(my_group + d, groups)
            pltpu.make_async_remote_copy(
                src_ref=mat_send.at[v, slab_of(g)], dst_ref=mat_recv.at[my_group, v],
                send_sem=mat_ssem, recv_sem=mat_rsem, device_id=(g, me), device_id_type=MESH,
            ).start()

    rest = pl.ds(0, groups - 1)
    pltpu.make_async_copy(lab_recv.at[rest], lab_recv.at[rest], fwd_rsem).wait()
    places = [place]
    for d in range(1, groups):
        places.append(positions(lax.rem(my_group + d, groups)))
    pltpu.make_async_copy(mat_recv.at[rest], mat_recv.at[rest], mat_rsem).wait()
    pltpu.make_async_copy(wgt_recv, wgt_recv, wgt_rsem).wait()

    for k in range(blocks):
        here = slice(k * width, (k + 1) * width)
        numer = jnp.zeros((slab, width), F32)
        denom = jnp.zeros((slab, width), F32)
        for d in range(groups):
            g = lax.rem(my_group + d, groups)
            for v in range(visits):
                weight = wgt_recv[g, places[d][v * blocks + k]].astype(F32)
                if d == 0:
                    matched = mat[v, slab_of(my_group), here]
                else:
                    matched = mat_recv[g, v, :, here].astype(F32)
                numer = numer + weight * matched
                denom = denom + weight
        out_ref[0, :, here] = numer / denom

    some = pl.ds(0, patches - 1)
    last = pl.ds(0, patches - 1 - first)
    pltpu.make_async_copy(img_send.at[last], img_send.at[last], img_ssem).wait()
    pltpu.make_async_copy(lab_send.at[some], lab_send.at[some], lab_ssem).wait()
    pltpu.make_async_copy(lab_recv.at[rest], lab_recv.at[rest], fwd_ssem).wait()
    pltpu.make_async_copy(wgt_recv.at[0, some], wgt_recv.at[0, some], wgt_osem).wait()
    pltpu.make_async_copy(wgt_recv.at[rest], wgt_recv.at[rest], wgt_ssem).wait()
    pltpu.make_async_copy(mat_recv.at[rest], mat_recv.at[rest], mat_ssem).wait()


def solution(mesh):
    groups, patches = mesh.shape["group"], mesh.shape["patch"]

    def per_device(strip_image, strip_weight, strip_patch, strip_slot, kernel_coef):
        _, strips, rows, width = strip_image.shape
        visits = kernel_coef.shape[2]
        cols = strips // visits * width
        slab = rows // groups
        vertical, horizontal = tables(rows, width)
        count = vertical.shape[0]
        far = pl.BlockSpec(memory_space=pltpu.HBM)
        coef = jnp.transpose(kernel_coef[0, 0], (1, 0, 2))
        dma = pltpu.SemaphoreType.DMA
        macs = visits * cols * rows * count * (2 * width + 2 * rows)
        return pl.pallas_call(
            functools.partial(kernel, groups, patches),
            out_shape=pltpu.VMEM((1, slab, cols), F32),
            in_specs=[far] * 7,
            out_specs=pl.BlockSpec(memory_space=pltpu.VMEM),
            scratch_shapes=[
                pltpu.SMEM(strip_patch.shape, jnp.int32),
                pltpu.SMEM(strip_slot.shape, jnp.int32),
                pltpu.SMEM(coef.shape, F32),
                pltpu.SMEM((2, patches), jnp.int32),
                pltpu.VMEM((strips, rows, width), BF16),
                pltpu.VMEM((strips, rows, width), BF16),
                pltpu.VMEM(vertical.shape, F32),
                pltpu.VMEM(horizontal.shape, BF16),
                pltpu.VMEM((patches, rows, width), BF16),
                pltpu.VMEM((patches, rows, width), BF16),
                pltpu.VMEM((patches, rows, width), BF16),
                pltpu.VMEM((groups, patches, slab, width), BF16),
                pltpu.VMEM((patches, 1, 128), jnp.int32),
                pltpu.VMEM((groups, patches, 1, 128), jnp.int32),
                pltpu.VMEM((strips * rows, 2 * width), BF16),
                pltpu.VMEM((visits, count * rows, cols), BF16),
                pltpu.VMEM((visits, 2 * rows, count * rows), BF16),
                pltpu.VMEM((visits, rows, cols), F32),
                pltpu.VMEM((visits, rows, cols), BF16),
                pltpu.VMEM((groups, visits, slab, cols), BF16),
                dma((7,)),
            ]
            + [dma] * 12,
            compiler_params=pltpu.CompilerParams(
                collective_id=0, has_side_effects=True, vmem_limit_bytes=48 * 1024 * 1024
            ),
            cost_estimate=pl.CostEstimate(flops=2 * macs, bytes_accessed=1 << 21, transcendentals=0),
        )(
            *[
                pltpu.with_memory_space_constraint(x, pltpu.HBM)
                for x in (
                    strip_patch, strip_slot, coef, strip_image, strip_weight,
                    jnp.asarray(vertical), jnp.asarray(horizontal),
                )
            ]
        )

    return jax.shard_map(
        per_device,
        mesh=mesh,
        in_specs=(
            P("group", "patch", None, None),
            P("group", "patch", None, None),
            P("group", "patch"),
            P("group", "patch"),
            P("group", "patch", None, None, None),
        ),
        out_specs=P("patch", "group", None),
        check_vma=False,
    )
```

```python
import functools

import jax
import jax.numpy as jnp
import ml_dtypes
import numpy as np
from jax import lax
from jax.experimental import pallas as pl
from jax.experimental.pallas import tpu as pltpu
from jax.sharding import PartitionSpec as P

TAPS = 23
HALF = 11
SPREADS = (0.7, 1.5, 3.0)
DEGREES = (4, 3, 2)
MESH = pl.DeviceIdType.MESH
F32 = jnp.float32
BF16 = jnp.bfloat16


def profile_table():
    offsets = np.arange(-HALF, HALF + 1).astype(np.float64)
    profiles = []
    for spread, degree in zip(SPREADS, DEGREES):
        for power in range(degree + 1):
            profile = np.exp(-offsets * offsets / (2.0 * spread * spread)) * (offsets / spread) ** power
            profiles.append(profile / np.sqrt(np.sum(profile * profile)))
    return np.stack(profiles).astype(np.float32).astype(ml_dtypes.bfloat16).astype(np.float32)


def basis_pairs():
    pairs, start = [], 0
    for degree in DEGREES:
        for vertical in range(degree + 1):
            for horizontal in range(degree + 1 - vertical):
                pairs.append((start + vertical, start + horizontal))
        start += degree + 1
    return pairs


def band(profile, inputs, outputs):
    differ = outputs[None, :] - inputs[:, None]
    return np.where(np.abs(differ) <= HALF, profile[np.clip(differ + HALF, 0, 2 * HALF)], 0.0)


def tables(rows, width):
    profiles = profile_table()
    y = np.arange(rows)
    vertical = np.stack([band(p, y, y).T for p in profiles])
    x = np.arange(width)
    halo = np.where(x < width // 2, x + width, x - width)
    lanes = np.concatenate([x, halo])
    horizontal = np.concatenate([band(p, lanes, x) for p in profiles], axis=1)
    return vertical.astype(np.float32), horizontal.astype(ml_dtypes.bfloat16)


def kernel(
    groups, patches,
    patch_hbm, slot_hbm, coef_hbm, img_hbm, wgt_hbm, ver_hbm, hor_hbm, out_ref,
    patch_ref, slot_ref, coef_ref, found,
    img_in, wgt_in, ver, band_h, img_send, img_recv, wgt_send, wgt_recv, lab_send, lab_recv,
    win, hor, mix, mat, mat_send, mat_recv,
    in_sem, lab_ssem, lab_rsem, fwd_ssem, fwd_rsem, img_fsem, img_ssem, img_rsem,
    wgt_ssem, wgt_osem, wgt_rsem, mat_ssem, mat_rsem,
):
    my_group, me = lax.axis_index("group"), lax.axis_index("patch")
    strips, rows, width = img_in.shape
    visits, cols = mat.shape[0], mat.shape[2]
    blocks = strips // visits
    slab = rows // groups
    count = ver.shape[0]
    devices = groups * patches

    loads = [
        pltpu.make_async_copy(src, dst, in_sem.at[i])
        for i, (src, dst) in enumerate(
            [
                (img_hbm.at[0], img_in), (wgt_hbm.at[0], wgt_in), (ver_hbm, ver), (hor_hbm, band_h),
                (patch_hbm, patch_ref), (slot_hbm, slot_ref), (coef_hbm, coef_ref),
            ]
        )
    ]
    for i in (4, 5, 0, 1, 6, 2, 3):
        loads[i].start()

    barrier = pltpu.get_barrier_semaphore()
    mine = my_group * patches + me

    def greet(i, carry):
        other = lax.rem(mine + 1 + i, devices)
        pl.semaphore_signal(
            barrier, inc=1, device_id=(other // patches, lax.rem(other, patches)), device_id_type=MESH
        )
        return carry

    lax.fori_loop(0, devices - 1, greet, 0)

    def find(p, carry):
        source, label = jnp.int32(0), jnp.int32(0)
        for s in range(strips):
            here = patch_ref[0, s] == p
            source = jnp.where(here, s, source)
            label = jnp.where(here, slot_ref[0, s] + 1, label)
        found[0, p] = source
        found[1, p] = label
        return carry

    def pack_label(p, carry):
        lab_send[p] = jnp.full((1, 128), found[1, p], jnp.int32)
        return carry

    def pack_image(p, carry):
        img_send[p] = img_in[found[0, p]]
        return carry

    def pack_weight(p, carry):
        wgt_send[p] = wgt_in[found[0, p]]
        return carry

    def other_patch(i):
        quarter = patches // 4
        lead = quarter - quarter // 4
        j = lax.div(i, 2)
        by_turns = lax.select(
            lax.rem(j - lead + quarter, 2) == 0, quarter + lax.div(j - lead, 2), lead + lax.div(j - lead, 2)
        )
        far = lax.select(j < lead, j, lax.select(j >= 2 * quarter - lead, j, by_turns))
        step = lax.select(lax.rem(i, 2) == 0, 2 * quarter + far, j + 1)
        other, bit = jnp.int32(0), 1
        while bit < patches:
            other = other + bit * lax.rem(lax.div(me, bit) + lax.div(step, bit), 2)
            bit *= 2
        return other

    loads[4].wait()
    loads[5].wait()
    lax.fori_loop(0, patches, find, 0)
    loads[0].wait()
    lax.fori_loop(0, patches, pack_image, 0)
    pl.semaphore_wait(barrier, devices - 1)

    def send_label(i, carry):
        p = other_patch(i)
        pltpu.make_async_remote_copy(
            src_ref=lab_send.at[p], dst_ref=lab_recv.at[my_group, me],
            send_sem=lab_ssem, recv_sem=lab_rsem, device_id=(my_group, p), device_id_type=MESH,
        ).start()
        return carry

    def send_image(i, carry, sem=img_ssem):
        p = other_patch(lax.select(i < patches // 2, 2 * i, 2 * (i - patches // 2) + 1))
        pltpu.make_async_remote_copy(
            src_ref=img_send.at[p], dst_ref=img_recv.at[me],
            send_sem=sem, recv_sem=img_rsem, device_id=(my_group, p), device_id_type=MESH,
        ).start()
        return carry

    first = patches // 4
    lax.fori_loop(0, first, functools.partial(send_image, sem=img_fsem), 0)
    lax.fori_loop(first, 2 * first, send_image, 0)
    lax.fori_loop(0, patches, pack_label, 0)
    lax.fori_loop(0, patches - 1, send_label, 0)
    pltpu.make_async_copy(lab_send.at[me], lab_recv.at[my_group, me], lab_rsem).start()
    lax.fori_loop(2 * first, patches - 1, send_image, 0)
    pltpu.make_async_copy(img_send.at[me], img_recv.at[me], img_rsem).start()

    loads[1].wait()
    lax.fori_loop(0, patches, pack_weight, 0)

    loads[2].wait()
    loads[6].wait()
    pairs = basis_pairs()
    down = (2.0 * lax.broadcasted_iota(jnp.int32, (rows, rows), 0).astype(F32) - (rows - 1)) / (rows - 1)

    def mix_visit(v, carry):
        for r in range(count):
            flat = jnp.zeros((rows, rows), F32)
            across = jnp.zeros((rows, rows), F32)
            tilt = jnp.zeros((rows, rows), F32)
            for b, (q, h) in enumerate(pairs):
                if h == r:
                    vertical = ver[q]
                    flat = flat + coef_ref[0, v, b] * vertical
                    across = across + coef_ref[1, v, b] * vertical
                    tilt = tilt + coef_ref[2, v, b] * vertical
            mix[v, :rows, r * rows : (r + 1) * rows] = (flat + down * tilt).astype(BF16)
            mix[v, rows:, r * rows : (r + 1) * rows] = across.astype(BF16)
        return carry

    lax.fori_loop(0, visits, mix_visit, 0)


    def slab_of(g):
        return pl.ds(pl.multiple_of(g * slab, slab), slab)

    def send_weight(i, carry):
        near = patches // 2 - 1
        p = other_patch(lax.select(i < near, 2 * i + 1, 2 * (i - near)))
        for d in range(groups):
            g = lax.rem(my_group + d, groups)
            pltpu.make_async_remote_copy(
                src_ref=wgt_send.at[p, slab_of(g)], dst_ref=wgt_recv.at[my_group, me],
                send_sem=wgt_osem if d == 0 else wgt_ssem, recv_sem=wgt_rsem,
                device_id=(g, p), device_id_type=MESH,
            ).start()
        return carry

    lax.fori_loop(0, patches - 1, send_weight, 0)
    pltpu.make_async_copy(wgt_send.at[me, slab_of(my_group)], wgt_recv.at[my_group, me], wgt_rsem).start()
    for d in range(1, groups):
        g = lax.rem(my_group + d, groups)
        pltpu.make_async_remote_copy(
            src_ref=wgt_send.at[me, slab_of(g)], dst_ref=wgt_recv.at[my_group, me],
            send_sem=wgt_ssem, recv_sem=wgt_rsem, device_id=(g, me), device_id_type=MESH,
        ).start()

    pltpu.make_async_copy(lab_recv.at[0], lab_recv.at[0], lab_rsem).wait()
    for d in range(1, groups):
        pltpu.make_async_remote_copy(
            src_ref=lab_recv.at[my_group], dst_ref=lab_recv.at[my_group],
            send_sem=fwd_ssem, recv_sem=fwd_rsem,
            device_id=(lax.rem(my_group + d, groups), me), device_id_type=MESH,
        ).start()

    def positions(g):
        labels = lab_recv[g]
        order = lax.broadcasted_iota(jnp.int32, labels.shape, 0)
        return [
            jnp.max(jnp.where(labels == t + 1, order, 0)) for t in range(strips)
        ]

    place = positions(my_group)
    pltpu.make_async_copy(img_recv, img_recv, img_rsem).wait()

    zeros = jnp.zeros((rows, width), BF16)
    half = width // 2
    for t in range(strips):
        k = t % blocks
        here = slice(t * rows, (t + 1) * rows)
        win[here, :width] = img_recv[place[t]]
        right = img_recv[place[t + 1]] if k < blocks - 1 else zeros
        left = img_recv[place[t - 1]] if k > 0 else zeros
        win[here, width : width + half] = right[:, :half]
        win[here, width + half :] = left[:, half:]

    loads[3].wait()
    per = 2
    for v in range(visits):
        for j in range(count // per):
            part = jnp.dot(
                win[v * blocks * rows : (v + 1) * blocks * rows, :],
                band_h[:, j * per * width : (j + 1) * per * width],
                preferred_element_type=F32,
            ).astype(BF16)
            for k in range(blocks):
                for i in range(per):
                    r = j * per + i
                    hor[v, r * rows : (r + 1) * rows, k * width : (k + 1) * width] = part[
                        k * rows : (k + 1) * rows, i * width : (i + 1) * width
                    ]

    chunk = 2 * width
    for v in range(visits):
        for c in range(cols // chunk):
            here = slice(c * chunk, (c + 1) * chunk)
            both = jnp.dot(mix[v], hor[v, :, here], preferred_element_type=F32)
            at = lax.broadcasted_iota(jnp.int32, (rows, chunk), 1).astype(F32) + c * chunk
            sideways = (2.0 * at - (cols - 1)) / (cols - 1)
            matched = both[:rows] + sideways * both[rows:]
            mat[v, :, here] = matched
            mat_send[v, :, here] = matched.astype(BF16)
        for d in range(1, groups):
            g = lax.rem(my_group + d, groups)
            pltpu.make_async_remote_copy(
                src_ref=mat_send.at[v, slab_of(g)], dst_ref=mat_recv.at[my_group, v],
                send_sem=mat_ssem, recv_sem=mat_rsem, device_id=(g, me), device_id_type=MESH,
            ).start()

    rest = pl.ds(0, groups - 1)
    pltpu.make_async_copy(lab_recv.at[rest], lab_recv.at[rest], fwd_rsem).wait()
    places = [place]
    for d in range(1, groups):
        places.append(positions(lax.rem(my_group + d, groups)))
    pltpu.make_async_copy(mat_recv.at[rest], mat_recv.at[rest], mat_rsem).wait()
    pltpu.make_async_copy(wgt_recv, wgt_recv, wgt_rsem).wait()

    for k in range(blocks):
        here = slice(k * width, (k + 1) * width)
        numer = jnp.zeros((slab, width), F32)
        denom = jnp.zeros((slab, width), F32)
        for d in range(groups):
            g = lax.rem(my_group + d, groups)
            for v in range(visits):
                weight = wgt_recv[g, places[d][v * blocks + k]].astype(F32)
                if d == 0:
                    matched = mat[v, slab_of(my_group), here]
                else:
                    matched = mat_recv[g, v, :, here].astype(F32)
                numer = numer + weight * matched
                denom = denom + weight
        out_ref[0, :, here] = numer / denom

    some = pl.ds(0, patches - 1)
    pltpu.make_async_copy(img_send.at[pl.ds(0, first)], img_send.at[pl.ds(0, first)], img_fsem).wait()
    last = pl.ds(0, patches - 1 - first)
    pltpu.make_async_copy(img_send.at[last], img_send.at[last], img_ssem).wait()
    pltpu.make_async_copy(lab_send.at[some], lab_send.at[some], lab_ssem).wait()
    pltpu.make_async_copy(lab_recv.at[rest], lab_recv.at[rest], fwd_ssem).wait()
    pltpu.make_async_copy(wgt_recv.at[0, some], wgt_recv.at[0, some], wgt_osem).wait()
    pltpu.make_async_copy(wgt_recv.at[rest], wgt_recv.at[rest], wgt_ssem).wait()
    pltpu.make_async_copy(mat_recv.at[rest], mat_recv.at[rest], mat_ssem).wait()


def solution(mesh):
    groups, patches = mesh.shape["group"], mesh.shape["patch"]

    def per_device(strip_image, strip_weight, strip_patch, strip_slot, kernel_coef):
        _, strips, rows, width = strip_image.shape
        visits = kernel_coef.shape[2]
        cols = strips // visits * width
        slab = rows // groups
        vertical, horizontal = tables(rows, width)
        count = vertical.shape[0]
        far = pl.BlockSpec(memory_space=pltpu.HBM)
        coef = jnp.transpose(kernel_coef[0, 0], (1, 0, 2))
        dma = pltpu.SemaphoreType.DMA
        macs = visits * cols * rows * count * (2 * width + 2 * rows)
        return pl.pallas_call(
            functools.partial(kernel, groups, patches),
            out_shape=pltpu.VMEM((1, slab, cols), F32),
            in_specs=[far] * 7,
            out_specs=pl.BlockSpec(memory_space=pltpu.VMEM),
            scratch_shapes=[
                pltpu.SMEM(strip_patch.shape, jnp.int32),
                pltpu.SMEM(strip_slot.shape, jnp.int32),
                pltpu.SMEM(coef.shape, F32),
                pltpu.SMEM((2, patches), jnp.int32),
                pltpu.VMEM((strips, rows, width), BF16),
                pltpu.VMEM((strips, rows, width), BF16),
                pltpu.VMEM(vertical.shape, F32),
                pltpu.VMEM(horizontal.shape, BF16),
                pltpu.VMEM((patches, rows, width), BF16),
                pltpu.VMEM((patches, rows, width), BF16),
                pltpu.VMEM((patches, rows, width), BF16),
                pltpu.VMEM((groups, patches, slab, width), BF16),
                pltpu.VMEM((patches, 1, 128), jnp.int32),
                pltpu.VMEM((groups, patches, 1, 128), jnp.int32),
                pltpu.VMEM((strips * rows, 2 * width), BF16),
                pltpu.VMEM((visits, count * rows, cols), BF16),
                pltpu.VMEM((visits, 2 * rows, count * rows), BF16),
                pltpu.VMEM((visits, rows, cols), F32),
                pltpu.VMEM((visits, rows, cols), BF16),
                pltpu.VMEM((groups, visits, slab, cols), BF16),
                dma((7,)),
            ]
            + [dma] * 12,
            compiler_params=pltpu.CompilerParams(
                collective_id=0, has_side_effects=True, vmem_limit_bytes=48 * 1024 * 1024
            ),
            cost_estimate=pl.CostEstimate(flops=2 * macs, bytes_accessed=1 << 21, transcendentals=0),
        )(
            *[
                pltpu.with_memory_space_constraint(x, pltpu.HBM)
                for x in (
                    strip_patch, strip_slot, coef, strip_image, strip_weight,
                    jnp.asarray(vertical), jnp.asarray(horizontal),
                )
            ]
        )

    return jax.shard_map(
        per_device,
        mesh=mesh,
        in_specs=(
            P("group", "patch", None, None),
            P("group", "patch", None, None),
            P("group", "patch"),
            P("group", "patch"),
            P("group", "patch", None, None, None),
        ),
        out_specs=P("patch", "group", None),
        check_vma=False,
    )
```
